32 devices in a mesh: node: 8 (over z, y), col: 4 (over x, core).
Axes of the slice: x: 2, y: 2, z: 4, core: 2. Of those that a mesh axis runs over, the one named last changes fastest.
Arguments:
- panel: bfloat16 [38912, 256], P('node', 'col'), may hold values from -6 to 6
- basis: bfloat16 [38912, 2048], P('node', 'col'), may hold values from -0.0390625 to 0.0390625
- g_blocks: bfloat16 [304, 3, 128, 128], P('node'), may hold values from -0.3125 to 0.3125
- c_blocks: bfloat16 [304, 3, 128, 128], P('node'), may hold values from -0.3125 to 0.3125
- block_cols: int32 [304, 3], P('node'), may hold values from 0 to 303, as said below
Outputs:
- reduced_g: float32 [2048, 256], P(('col', 'node'))
- reduced_c: float32 [2048, 256], P(('col', 'node'))
The draws below stay inside these ranges and needn't reach their ends.
Inputs may be any that keep to these rules, and one draw needn't show every extreme that they name: `block_cols`: block row i names block columns within 4 of i: the first is i itself, and one lies exactly 4 away wherever that stays inside the grid.
All inputs are finite; a program needn't handle non-finite values.
Results may differ from the reference program's by a relative error of at most 0.0029.
Values may be sent and summed in bfloat16 or wider, within the bound.
No kernel may reach another device: no remote copies, remote signals or barrier semaphores. Data moves between devices by JAX's collectives and lax.ppermute only.
A program may use at most 64 MiB of HBM per device.

```python
import jax
import jax.numpy as jnp
from jax import lax

BS = 128
SLOTS = 3
HB = 4
K = 256
Q = 2048
NB = 304
N = 38912


def draw_block_cols(key, part):
    first_key, second_key = jax.random.split(jax.random.fold_in(key, 17))
    row_ids = jnp.arange(NB, dtype=jnp.int32)
    nearby = jax.random.randint(first_key, (NB,), -HB, HB + 1).astype(jnp.int32)
    sides = (jax.random.randint(second_key, (NB,), 0, 2) * 2 - 1).astype(jnp.int32)
    stacked = jnp.stack([row_ids, row_ids + nearby, row_ids + sides * HB], 1)
    return jnp.clip(stacked, 0, NB - 1).astype(jnp.int32)


def raised(drawn, key, source, target, blocks, factor):
    def block_of(dim):
        return (jnp.arange(drawn.shape[dim]) // (drawn.shape[dim] // blocks)).reshape((-1,) + (1,) * (drawn.ndim - 1 - dim))

    first = jax.random.permutation(key, blocks)[block_of(target)]
    second = (block_of(target) + blocks // 2) % blocks
    return jnp.where((block_of(source) == first) | (block_of(source) == second), factor * drawn, drawn)


def levels(key, extent, shards, least, high):
    def one(axis_at, shards_of):
        steps = jax.random.uniform(jax.random.fold_in(jax.random.fold_in(key, 6), axis_at), (shards_of,), jnp.float32, least / len(shards), high / len(shards))
        return jnp.repeat(jnp.exp(steps), extent[axis_at] // shards_of).reshape((-1,) + (1,) * (len(extent) - axis_at - 1))

    factor_of = one(*shards[0])
    for cut in shards[1:]:
        factor_of = factor_of * one(*cut)
    return factor_of


def centred(own_key, extent, width, reach, cuts=(), kind=jnp.bfloat16):
    loudness = levels(own_key, extent, cuts, -0.22, 0.18) if cuts else 1.0
    values = jax.random.normal(own_key, extent, jnp.float32) * width * loudness
    return jnp.minimum(jnp.maximum(values, -reach), reach).astype(kind)


def gaussian_with(stream_key, extent, spread, limit, cuts, heavy, kind=jnp.bfloat16):
    values = spread * jax.random.normal(stream_key, extent, jnp.float32)
    if cuts:
        values = values * levels(stream_key, extent, cuts, -0.22, 0.18)
    return jnp.clip(raised(values, jax.random.fold_in(stream_key, 3), *heavy), -limit, limit).astype(kind)


def setup_inputs(seed: int = 0) -> dict:
    streams_of = jax.random.split(jax.random.key(seed), 6)
    return {
        "panel": centred(streams_of[0], (N, K), 1.0, 6.0, ((0, 8), (1, 4))),
        "basis": gaussian_with(streams_of[1], (N, Q), N ** -0.5, 0.0390625, ((0, 8), (1, 4)), (0, 1, 8, 2.0)),
        "g_blocks": centred(streams_of[2], (NB, SLOTS, BS, BS), (SLOTS * BS) ** -0.5, 0.3125, ((0, 8),)),
        "c_blocks": centred(streams_of[3], (NB, SLOTS, BS, BS), (SLOTS * BS) ** -0.5, 0.3125, ((0, 8),)),
        "block_cols": draw_block_cols(jax.random.fold_in(streams_of[5], 71), 0),
    }


def multiply(blocks, pieces, block_cols):
    block_rows = pieces.shape[0]
    summed = jnp.zeros(pieces.shape, jnp.float32)
    for slot_idx in range(SLOTS):
        nearby = pieces[block_cols[:, slot_idx]].astype(jnp.float32)
        summed = summed + jnp.einsum('rab,rbk->rak', blocks[:, slot_idx].astype(jnp.float32), nearby)
    return summed.reshape(block_rows * pieces.shape[1], pieces.shape[2]).astype(jnp.bfloat16)


def reference(panel, basis, g_blocks, c_blocks, block_cols):
    block_rows = block_cols.shape[0]
    pieces = panel.reshape(block_rows, g_blocks.shape[2], panel.shape[1])
    y_g = multiply(g_blocks, pieces, block_cols)
    y_c = multiply(c_blocks, pieces, block_cols)
    dims = (((0,), (0,)), ((), ()))
    reduced_g = lax.dot_general(basis, y_g, dims, preferred_element_type=jnp.float32)
    reduced_c = lax.dot_general(basis, y_c, dims, preferred_element_type=jnp.float32)
    return (reduced_g, reduced_c)
```

```python
import functools

import jax
import jax.numpy as jnp
from jax import lax
from jax.experimental import pallas as pl
from jax.experimental.pallas import tpu as pltpu
from jax.sharding import PartitionSpec as P

BS = 128
HB = 4
F32 = jnp.float32
BF16 = jnp.bfloat16


def cuts(total, parts):
    edges = [total * i // parts for i in range(parts + 1)]
    return list(zip(edges[:-1], edges[1:]))


def project_kernel(groups, ids_ref, mine, other, low_m, high_m, low_o, high_o, g_hbm, c_hbm, basis_hbm,
                   send_ref, keep_ref, ext, g_buf, c_buf, b_buf, yt, acc, sems):
    rows = g_hbm.shape[0]
    slots = g_hbm.shape[1]
    width = mine.shape[0]
    inner = mine.shape[1]
    halo = HB * BS
    node = lax.axis_index("node")
    core = lax.axis_index("col") % 2
    spans = cuts(rows, 4)

    copies = []
    for step, (lo, hi) in enumerate(spans):
        span = pl.ds(lo, hi - lo)
        nodes = pl.ds(lo * BS, (hi - lo) * BS)
        batch = [
            pltpu.make_async_copy(g_hbm.at[span], g_buf.at[span], sems.at[step, 0]),
            pltpu.make_async_copy(c_hbm.at[span], c_buf.at[span], sems.at[step, 1]),
            pltpu.make_async_copy(basis_hbm.at[nodes], b_buf.at[nodes], sems.at[step, 2]),
        ]
        for copy in batch:
            copy.start()
        copies.append(batch)

    for place, low, middle, high in ((core, low_m, mine, high_m), (1 - core, low_o, other, high_o)):
        at = pl.ds(pl.multiple_of(place * width, width), width)
        ext[at, 0:halo] = low[...]
        ext[at, halo:halo + inner] = middle[...]
        ext[at, halo + inner:] = high[...]

    offset = node * rows - HB
    for step, (lo, hi) in enumerate(spans):
        for copy in copies[step]:
            copy.wait()
        for row in range(lo, hi):
            near = []
            for slot in range(slots):
                local = jnp.clip(ids_ref[slot, row] - offset, 0, rows + 2 * HB - 1)
                near.append(ext[:, pl.ds(pl.multiple_of(local * BS, BS), BS)])
            near = jnp.concatenate(near, axis=1)
            both = jnp.concatenate(
                [
                    jnp.concatenate([g_buf[row, slot] for slot in range(slots)], axis=1),
                    jnp.concatenate([c_buf[row, slot] for slot in range(slots)], axis=1),
                ],
                axis=0,
            )
            prod = lax.dot_general(near, both, (((1,), (1,)), ((), ())), preferred_element_type=F32)
            prod = prod.astype(BF16)
            yt[0:2 * width, row * BS:(row + 1) * BS] = prod[:, 0:BS]
            yt[2 * width:4 * width, row * BS:(row + 1) * BS] = prod[:, BS:2 * BS]
        part = jnp.dot(yt[:, lo * BS:hi * BS], b_buf[lo * BS:hi * BS, :], preferred_element_type=F32)
        if step == 0:
            acc[...] = part
        else:
            acc[...] += part
    total = acc[...].T
    states, columns = total.shape
    total = total.reshape(groups, 2, states // (2 * groups), columns)
    odd = node % 2 == 1
    keep_ref[...] = jnp.where(odd, total[:, 1], total[:, 0])
    send_ref[...] = jnp.where(odd, total[:, 0], total[:, 1]).astype(BF16)


def project(ids, mine, other, halos_m, halos_o, g_blocks, c_blocks, basis, groups):
    rows, slots = g_blocks.shape[0], g_blocks.shape[1]
    width, inner = mine.shape
    states = basis.shape[1]
    piece = (groups, states // (2 * groups), 4 * width)
    vmem = pl.BlockSpec(memory_space=pltpu.VMEM)
    hbm = pl.BlockSpec(memory_space=pl.ANY)
    flops = 2 * rows * BS * 4 * width * (slots * BS + states)
    return pl.pallas_call(
        functools.partial(project_kernel, groups),
        out_shape=(jax.ShapeDtypeStruct(piece, BF16), jax.ShapeDtypeStruct(piece, F32)),
        in_specs=[pl.BlockSpec(memory_space=pltpu.SMEM)] + [vmem] * 6 + [hbm] * 3,
        out_specs=(vmem, vmem),
        scratch_shapes=[
            pltpu.VMEM((2 * width, inner + 2 * HB * BS), BF16),
            pltpu.VMEM(g_blocks.shape, BF16),
            pltpu.VMEM(c_blocks.shape, BF16),
            pltpu.VMEM(basis.shape, BF16),
            pltpu.VMEM((4 * width, inner), BF16),
            pltpu.VMEM((4 * width, states), F32),
            pltpu.SemaphoreType.DMA((4, 3)),
        ],
        compiler_params=pltpu.CompilerParams(vmem_limit_bytes=40 * 1024 * 1024),
        cost_estimate=pl.CostEstimate(flops=flops, bytes_accessed=14_000_000, transcendentals=0),
    )(ids, mine, other, *halos_m, *halos_o, g_blocks, c_blocks, basis)


def spread_kernel(groups, keep_a, got_a, keep_b, got_b, keep_ref, *send_refs):
    here = lax.axis_index("node") // 2
    half = keep_a.shape[2]
    for step in range(groups):
        at = here ^ step
        for lo, keep, got in ((0, keep_a, got_a), (half, keep_b, got_b)):
            value = keep[at] + got[at].astype(F32)
            if step == 0:
                keep_ref[:, lo:lo + half] = value
            else:
                send_refs[step - 1][:, lo:lo + half] = value.astype(BF16)


def spread(groups, keep_a, got_a, keep_b, got_b):
    piece = (keep_a.shape[1], 2 * keep_a.shape[2])
    vmem = pl.BlockSpec(memory_space=pltpu.VMEM)
    return pl.pallas_call(
        functools.partial(spread_kernel, groups),
        out_shape=[jax.ShapeDtypeStruct(piece, F32)] + [jax.ShapeDtypeStruct(piece, BF16)] * (groups - 1),
        in_specs=[vmem] * 4,
        out_specs=[vmem] * groups,
    )(keep_a, got_a, keep_b, got_b)


def finish_kernel(keep, *refs):
    got, (out_g, out_c) = refs[:-2], refs[-2:]
    total = keep[...]
    for ref in got:
        total = total + ref[...].astype(F32)
    first = lax.axis_index("col") // 2
    quarter = total.shape[1] // 4
    for place, base in ((first, 0), (1 - first, 2 * quarter)):
        at = pl.ds(pl.multiple_of(place * quarter, quarter), quarter)
        out_g[:, at] = total[:, base:base + quarter]
        out_c[:, at] = total[:, base + quarter:base + 2 * quarter]


def finish(keep, got):
    piece = jax.ShapeDtypeStruct((keep.shape[0], keep.shape[1] // 2), F32)
    vmem = pl.BlockSpec(memory_space=pltpu.VMEM)
    return pl.pallas_call(
        finish_kernel,
        out_shape=(piece, piece),
        in_specs=[vmem] * (1 + len(got)),
        out_specs=(vmem, vmem),
    )(keep, *got)


def body(panel, basis, g_blocks, c_blocks, block_cols):
    nodes, cols = lax.axis_size("node"), lax.axis_size("col")
    groups = nodes // 2
    halo = HB * BS
    ids = block_cols.T
    mine = panel.T
    across = [(i, i ^ 2) for i in range(cols)]
    cores = [(i, i ^ 1) for i in range(cols)]
    up = [(i, i + 1) for i in range(nodes - 1)]
    down = [(i + 1, i) for i in range(nodes - 1)]
    pairs = [(i, i ^ 1) for i in range(nodes)]

    far = lax.ppermute(mine, "col", across)
    other = lax.ppermute(mine, "col", cores)
    low = lax.ppermute(mine[:, -halo:], "node", up)
    high = lax.ppermute(mine[:, :halo], "node", down)
    halos = jnp.concatenate([low, high], axis=1)
    far_halos = lax.ppermute(halos, "col", across)
    other_halos = lax.ppermute(halos, "col", cores)

    def sides(both):
        return both[:, :halo], both[:, halo:]

    send_a, keep_a = project(ids, mine, other, (low, high), sides(other_halos), g_blocks, c_blocks, basis, groups)
    got_a = lax.ppermute(send_a, "node", pairs)
    far_other = lax.ppermute(far, "col", cores)
    far_other_halos = lax.ppermute(far_halos, "col", cores)
    send_b, keep_b = project(
        ids, far, far_other, sides(far_halos), sides(far_other_halos), g_blocks, c_blocks, basis, groups
    )
    got_b = lax.ppermute(send_b, "node", pairs)
    keep, *sends = spread(groups, keep_a, got_a, keep_b, got_b)
    got = []
    for step, send in enumerate(sends, 1):
        got.append(lax.ppermute(send, "node", [(i, i ^ (2 * step)) for i in range(nodes)]))
    return finish(keep, got)


def solution(mesh):
    in_specs = (
        P("node", "col"),
        P("node", "col"),
        P("node", None, None, None),
        P("node", None, None, None),
        P("node", None),
    )
    out_specs = (P(("col", "node"), None), P(("col", "node"), None))
    return jax.shard_map(body, mesh=mesh, in_specs=in_specs, out_specs=out_specs, check_vma=False)
```

```python
import functools

import jax
import jax.numpy as jnp
from jax import lax
from jax.experimental import pallas as pl
from jax.experimental.pallas import tpu as pltpu
from jax.sharding import PartitionSpec as P

BS = 128
HB = 4
MIB = 1024 * 1024
F32 = jnp.float32
BF16 = jnp.bfloat16


def cuts(total, parts):
    edges = [total * i // parts for i in range(parts + 1)]
    return list(zip(edges[:-1], edges[1:]))


def load_kernel(*refs):
    count = len(refs) // 2
    sources, targets, sems = refs[:count], refs[count:2 * count], refs[-1]
    copies = []
    for which, (source, target) in enumerate(zip(sources, targets)):
        for part, (lo, hi) in enumerate(cuts(source.shape[0], 2)):
            span = pl.ds(lo, hi - lo)
            copies.append(pltpu.make_async_copy(source.at[span], target.at[span], sems.at[which, part]))
    for copy in copies:
        copy.start()
    for copy in copies:
        copy.wait()


def load(*arrays):
    hbm = pl.BlockSpec(memory_space=pltpu.HBM)
    anywhere = pl.BlockSpec(memory_space=pl.ANY)
    size = sum(array.size * array.dtype.itemsize for array in arrays)
    return pl.pallas_call(
        load_kernel,
        out_shape=[jax.ShapeDtypeStruct(array.shape, array.dtype) for array in arrays],
        in_specs=[hbm] * len(arrays),
        out_specs=[anywhere] * len(arrays),
        scratch_shapes=[pltpu.SemaphoreType.DMA((len(arrays), 2))],
        compiler_params=pltpu.CompilerParams(vmem_limit_bytes=44 * MIB),
        cost_estimate=pl.CostEstimate(flops=0, bytes_accessed=size // 100, transcendentals=0),
    )(*arrays)


def project_kernel(groups, ids_ref, mine, other, low_m, high_m, low_o, high_o, g_ref, c_ref, basis_ref,
                   send_ref, keep_ref, ext, prods):
    rows, slots = g_ref.shape[0], g_ref.shape[1]
    width, inner = mine.shape
    halo = HB * BS
    node = lax.axis_index("node")
    core = lax.axis_index("col") % 2

    for place, low, middle, high in ((core, low_m, mine, high_m), (1 - core, low_o, other, high_o)):
        at = pl.ds(pl.multiple_of(place * width, width), width)
        ext[at, 0:halo] = low[...]
        ext[at, halo:halo + inner] = middle[...]
        ext[at, halo + inner:] = high[...]

    offset = node * rows - HB
    for row in range(rows):
        near = []
        for slot in range(slots):
            local = jnp.clip(ids_ref[slot, row] - offset, 0, rows + 2 * HB - 1)
            near.append(ext[:, pl.ds(pl.multiple_of(local * BS, BS), BS)])
        near = jnp.concatenate(near, axis=1)
        both = jnp.concatenate(
            [jnp.concatenate([ref[row, slot] for slot in range(slots)], axis=1) for ref in (g_ref, c_ref)], axis=0
        )
        prod = lax.dot_general(both, near, (((1,), (1,)), ((), ())), preferred_element_type=F32).astype(BF16)
        prods[row * BS:(row + 1) * BS, 0:2 * width] = prod[0:BS]
        prods[row * BS:(row + 1) * BS, 2 * width:4 * width] = prod[BS:2 * BS]
    total = lax.dot_general(
        basis_ref[...], prods[...], (((0,), (0,)), ((), ())), preferred_element_type=F32
    )
    states, columns = total.shape
    total = total.reshape(groups, 2, states // (2 * groups), columns)
    odd = node % 2 == 1
    keep_ref[...] = jnp.where(odd, total[:, 1], total[:, 0])
    send_ref[...] = jnp.where(odd, total[:, 0], total[:, 1]).astype(BF16)


def project(ids, mine, other, halos_m, halos_o, g_blocks, c_blocks, basis, groups):
    rows, slots = g_blocks.shape[0], g_blocks.shape[1]
    width, inner = mine.shape
    states = basis.shape[1]
    piece = (groups, states // (2 * groups), 4 * width)
    vmem = pl.BlockSpec(memory_space=pltpu.VMEM)
    flops = 2 * rows * BS * 4 * width * (slots * BS + states)
    return pl.pallas_call(
        functools.partial(project_kernel, groups),
        out_shape=(jax.ShapeDtypeStruct(piece, BF16), jax.ShapeDtypeStruct(piece, F32)),
        in_specs=[pl.BlockSpec(memory_space=pltpu.SMEM)] + [vmem] * 9,
        out_specs=(vmem, vmem),
        scratch_shapes=[
            pltpu.VMEM((2 * width, inner + 2 * HB * BS), BF16),
            pltpu.VMEM((inner, 4 * width), BF16),
        ],
        compiler_params=pltpu.CompilerParams(vmem_limit_bytes=14 * MIB),
        cost_estimate=pl.CostEstimate(flops=flops // 100, bytes_accessed=0, transcendentals=0),
    )(ids, mine, other, *halos_m, *halos_o, g_blocks, c_blocks, basis)


def spread_kernel(groups, keep_a, got_a, keep_b, got_b, keep_ref, *send_refs):
    here = lax.axis_index("node") // 2
    half = keep_a.shape[2]
    for step in range(groups):
        at = here ^ step
        for lo, keep, got in ((0, keep_a, got_a), (half, keep_b, got_b)):
            value = keep[at] + got[at].astype(F32)
            if step == 0:
                keep_ref[:, lo:lo + half] = value
            else:
                send_refs[step - 1][:, lo:lo + half] = value.astype(BF16)


def spread(groups, keep_a, got_a, keep_b, got_b):
    piece = (keep_a.shape[1], 2 * keep_a.shape[2])
    vmem = pl.BlockSpec(memory_space=pltpu.VMEM)
    return pl.pallas_call(
        functools.partial(spread_kernel, groups),
        out_shape=[jax.ShapeDtypeStruct(piece, F32)] + [jax.ShapeDtypeStruct(piece, BF16)] * (groups - 1),
        in_specs=[vmem] * 4,
        out_specs=[vmem] * groups,
        compiler_params=pltpu.CompilerParams(vmem_limit_bytes=4 * MIB),
    )(keep_a, got_a, keep_b, got_b)


def finish_kernel(keep, *refs):
    got, (out_g, out_c) = refs[:-2], refs[-2:]
    total = keep[...]
    for ref in got:
        total = total + ref[...].astype(F32)
    first = lax.axis_index("col") // 2
    quarter = total.shape[1] // 4
    for place, base in ((first, 0), (1 - first, 2 * quarter)):
        at = pl.ds(pl.multiple_of(place * quarter, quarter), quarter)
        out_g[:, at] = total[:, base:base + quarter]
        out_c[:, at] = total[:, base + quarter:base + 2 * quarter]


def finish(keep, got):
    piece = jax.ShapeDtypeStruct((keep.shape[0], keep.shape[1] // 2), F32)
    vmem = pl.BlockSpec(memory_space=pltpu.VMEM)
    return pl.pallas_call(
        finish_kernel,
        out_shape=(piece, piece),
        in_specs=[vmem] * (1 + len(got)),
        out_specs=(vmem, vmem),
        compiler_params=pltpu.CompilerParams(vmem_limit_bytes=4 * MIB),
    )(keep, *got)


def body(panel, basis, g_blocks, c_blocks, block_cols):
    nodes, cols = lax.axis_size("node"), lax.axis_size("col")
    groups = nodes // 2
    halo = HB * BS
    ids = block_cols.T
    mine = panel.T
    across = [(i, i ^ 2) for i in range(cols)]
    cores = [(i, i ^ 1) for i in range(cols)]
    up = [(i, i + 1) for i in range(nodes - 1)]
    down = [(i + 1, i) for i in range(nodes - 1)]
    pairs = [(i, i ^ 1) for i in range(nodes)]

    far = lax.ppermute(mine, "col", across)
    other = lax.ppermute(mine, "col", cores)
    last, first, other = lax.optimization_barrier((mine[:, -halo:], mine[:, :halo], other))
    low = lax.ppermute(last, "node", up)
    high = lax.ppermute(first, "node", down)
    g_blocks, c_blocks, basis = load(g_blocks, c_blocks, basis)
    low, high, g_blocks, c_blocks, basis = lax.optimization_barrier((low, high, g_blocks, c_blocks, basis))
    halos = jnp.concatenate([low, high], axis=1)
    far_halos = lax.ppermute(halos, "col", across)
    other_halos = lax.ppermute(halos, "col", cores)

    def sides(both):
        return both[:, :halo], both[:, halo:]

    send_a, keep_a = project(ids, mine, other, (low, high), sides(other_halos), g_blocks, c_blocks, basis, groups)
    far, send_a = lax.optimization_barrier((far, send_a))
    got_a = lax.ppermute(send_a, "node", pairs)
    far_other = lax.ppermute(far, "col", cores)
    far_other_halos = lax.ppermute(far_halos, "col", cores)
    send_b, keep_b = project(
        ids, far, far_other, sides(far_halos), sides(far_other_halos), g_blocks, c_blocks, basis, groups
    )
    got_b = lax.ppermute(send_b, "node", pairs)
    keep, *sends = spread(groups, keep_a, got_a, keep_b, got_b)
    got = []
    for step, send in enumerate(sends, 1):
        got.append(lax.ppermute(send, "node", [(i, i ^ (2 * step)) for i in range(nodes)]))
    return finish(keep, got)


def solution(mesh):
    in_specs = (
        P("node", "col"),
        P("node", "col"),
        P("node", None, None, None),
        P("node", None, None, None),
        P("node", None),
    )
    out_specs = (P(("col", "node"), None), P(("col", "node"), None))
    return jax.shard_map(body, mesh=mesh, in_specs=in_specs, out_specs=out_specs, check_vma=False)
```

```python
import functools

import jax
import jax.numpy as jnp
from jax import lax
from jax.experimental import pallas as pl
from jax.experimental.pallas import tpu as pltpu
from jax.sharding import PartitionSpec as P

BS = 128
HB = 4
MIB = 1024 * 1024
F32 = jnp.float32
BF16 = jnp.bfloat16
VMEM = pl.BlockSpec(memory_space=pltpu.VMEM)
SMEM = pl.BlockSpec(memory_space=pltpu.SMEM)
HBM = pl.BlockSpec(memory_space=pl.ANY)


def params(mib):
    return pltpu.CompilerParams(vmem_limit_bytes=mib * MIB)


def shape(dims, kind):
    return jax.ShapeDtypeStruct(dims, kind)


def cut_kernel(half, panel, ends, first, last, front, sems):
    width, inner = panel.shape
    halo = HB * BS
    copies = [
        (panel.at[:, 0:halo], ends.at[:, 0:halo]),
        (panel.at[:, inner - halo:inner], ends.at[:, halo:2 * halo]),
        (panel.at[:, 0:halo], first),
        (panel.at[:, inner - halo:inner], last),
        (panel.at[:, halo:half], front),
    ]
    copies = [pltpu.make_async_copy(*pair, sems.at[i]) for i, pair in enumerate(copies)]
    for copy in copies:
        copy.start()
    for copy in copies:
        copy.wait()


def cut(panel, half):
    width, inner = panel.shape
    halo = HB * BS
    widths = (2 * halo, halo, halo, half - halo)
    return pl.pallas_call(
        functools.partial(cut_kernel, half),
        out_shape=[shape((width, w), BF16) for w in widths],
        in_specs=[HBM],
        out_specs=[VMEM] * 4,
        scratch_shapes=[pltpu.SemaphoreType.DMA((5,))],
        compiler_params=params(44),
    )(panel)


def load_kernel(*refs):
    count = len(refs) // 2
    sources, targets, sems = refs[:count], refs[count:2 * count], refs[-1]
    copies = []
    for which, (source, target) in enumerate(zip(sources, targets)):
        middle = source.shape[0] // 2
        for part, span in enumerate((pl.ds(0, middle), pl.ds(middle, source.shape[0] - middle))):
            copies.append(pltpu.make_async_copy(source.at[span], target.at[span], sems.at[which, part]))
    for copy in copies:
        copy.start()
    for copy in copies:
        copy.wait()


def load(*arrays):
    size = sum(array.size * array.dtype.itemsize for array in arrays)
    return pl.pallas_call(
        load_kernel,
        out_shape=[shape(array.shape, array.dtype) for array in arrays],
        in_specs=[HBM] * len(arrays),
        out_specs=[VMEM] * len(arrays),
        scratch_shapes=[pltpu.SemaphoreType.DMA((len(arrays), 2))],
        compiler_params=params(48),
        cost_estimate=pl.CostEstimate(flops=0, bytes_accessed=size, transcendentals=0),
    )(*arrays)


def project_kernel(spans, places, groups, more, *refs):
    ids_ref, g_ref, c_ref, basis_ref = refs[:4]
    pieces = refs[4:4 + 2 * len(places)]
    rest = list(refs[4 + 2 * len(places):])
    before = rest.pop(0) if more else None
    *outs, ext, prods = rest
    rows, slots = g_ref.shape[0], g_ref.shape[1]
    width = pieces[0].shape[0]
    node = lax.axis_index("node")
    core = lax.axis_index("col") % 2

    for which, parts in enumerate(places):
        for owner, ref in ((core, pieces[2 * which]), (1 - core, pieces[2 * which + 1])):
            at = pl.ds(pl.multiple_of(owner * width, width), width)
            for source, target, count in parts:
                ext[at, target:target + count] = ref[:, source:source + count]

    offset = node * rows - HB
    at = 0
    total = None
    for lo, hi in spans:
        begin = at
        for row in range(lo, hi):
            near = []
            for slot in range(slots):
                local = jnp.clip(ids_ref[slot, row] - offset, 0, rows + 2 * HB - 1)
                near.append(ext[:, pl.ds(pl.multiple_of(local * BS, BS), BS)])
            near = jnp.concatenate(near, axis=1)
            both = jnp.concatenate(
                [jnp.concatenate([ref[row, slot] for slot in range(slots)], axis=1) for ref in (g_ref, c_ref)], axis=0
            )
            prod = lax.dot_general(both, near, (((1,), (1,)), ((), ())), preferred_element_type=F32).astype(BF16)
            prods[at:at + BS, 0:2 * width] = prod[0:BS]
            prods[at:at + BS, 2 * width:4 * width] = prod[BS:2 * BS]
            at += BS
        part = lax.dot_general(
            basis_ref[lo * BS:hi * BS, :], prods[begin:at, :], (((0,), (0,)), ((), ())), preferred_element_type=F32
        )
        total = part if total is None else total + part
    if before is not None:
        total = total + before[...]
    if len(outs) == 1:
        outs[0][...] = total
        return
    send_ref, keep_ref = outs
    states, columns = total.shape
    total = total.reshape(groups, 2, states // (2 * groups), columns)
    odd = node % 2 == 1
    keep_ref[...] = jnp.where(odd, total[:, 1], total[:, 0])
    send_ref[...] = jnp.where(odd, total[:, 0], total[:, 1]).astype(BF16)


def project(fixed, pieces, spans, groups, before=None, last=True):
    ids, g_blocks, c_blocks, basis = fixed
    rows, slots = g_blocks.shape[0], g_blocks.shape[1]
    width = pieces[0][0].shape[0]
    states = basis.shape[1]
    piece = (groups, states // (2 * groups), 4 * width)
    whole = shape((states, 4 * width), F32)
    arrays = [array for mine, other, _ in pieces for array in (mine, other)]
    more = [] if before is None else [before]
    count = sum(hi - lo for lo, hi in spans)
    return pl.pallas_call(
        functools.partial(project_kernel, spans, [parts for _, _, parts in pieces], groups, before is not None),
        out_shape=(shape(piece, BF16), shape(piece, F32)) if last else (whole,),
        in_specs=[SMEM] + [VMEM] * (3 + len(arrays) + len(more)),
        out_specs=(VMEM, VMEM) if last else (VMEM,),
        scratch_shapes=[
            pltpu.VMEM((2 * width, (rows + 2 * HB) * BS), BF16),
            pltpu.VMEM((count * BS, 4 * width), BF16),
        ],
        compiler_params=params(14),
        cost_estimate=pl.CostEstimate(flops=count, bytes_accessed=count, transcendentals=0),
    )(ids, g_blocks, c_blocks, basis, *arrays, *more)


def spread_kernel(groups, keep_a, got_a, keep_b, got_b, keep_ref, *send_refs):
    here = lax.axis_index("node") // 2
    half = keep_a.shape[2]
    for step in range(groups):
        at = here ^ step
        for lo, keep, got in ((0, keep_a, got_a), (half, keep_b, got_b)):
            value = keep[at] + got[at].astype(F32)
            if step == 0:
                keep_ref[:, lo:lo + half] = value
            else:
                send_refs[step - 1][:, lo:lo + half] = value.astype(BF16)


def spread(groups, keep_a, got_a, keep_b, got_b):
    piece = (keep_a.shape[1], 2 * keep_a.shape[2])
    return pl.pallas_call(
        functools.partial(spread_kernel, groups),
        out_shape=[shape(piece, F32)] + [shape(piece, BF16)] * (groups - 1),
        in_specs=[VMEM] * 4,
        out_specs=[VMEM] * groups,
        compiler_params=params(4),
    )(keep_a, got_a, keep_b, got_b)


def finish_kernel(keep, *refs):
    got, (out_g, out_c) = refs[:-2], refs[-2:]
    total = keep[...]
    for ref in got:
        total = total + ref[...].astype(F32)
    first = lax.axis_index("col") // 2
    quarter = total.shape[1] // 4
    for place, base in ((first, 0), (1 - first, 2 * quarter)):
        at = pl.ds(pl.multiple_of(place * quarter, quarter), quarter)
        out_g[:, at] = total[:, base:base + quarter]
        out_c[:, at] = total[:, base + quarter:base + 2 * quarter]


def finish(keep, got):
    piece = shape((keep.shape[0], keep.shape[1] // 2), F32)
    return pl.pallas_call(
        finish_kernel,
        out_shape=(piece, piece),
        in_specs=[VMEM] * (1 + len(got)),
        out_specs=(VMEM, VMEM),
        compiler_params=params(4),
    )(keep, *got)


def body(panel, basis, g_blocks, c_blocks, block_cols):
    nodes, cols = lax.axis_size("node"), lax.axis_size("col")
    rows = g_blocks.shape[0]
    groups = nodes // 2
    halo = HB * BS
    inner = rows * BS
    half = inner - halo
    ids = block_cols.T
    mine = panel.T

    def across(array):
        return lax.ppermute(array, "col", [(i, i ^ 2) for i in range(cols)])

    def cores(array):
        return lax.ppermute(array, "col", [(i, i ^ 1) for i in range(cols)])

    def up(array):
        return lax.ppermute(array, "node", [(i, i + 1) for i in range(nodes - 1)])

    def down(array):
        return lax.ppermute(array, "node", [(i + 1, i) for i in range(nodes - 1)])

    def swap(array, step):
        return lax.ppermute(array, "node", [(i, i ^ step) for i in range(nodes)])

    other = cores(mine)
    ends, first, last, front = cut(mine, half)
    far_ends, far_front = across(ends), across(front)
    other, first, last = lax.optimization_barrier((other, first, last))
    low, high = up(last), down(first)
    (basis,), (g_blocks,), (c_blocks,) = load(basis), load(g_blocks), load(c_blocks)
    far_ends, g_blocks, c_blocks, basis = lax.optimization_barrier((far_ends, g_blocks, c_blocks, basis))
    fixed = (ids, g_blocks, c_blocks, basis)
    far_low, far_high = up(far_ends[:, halo:]), down(far_ends[:, :halo])
    middle = [(mine, other, [(0, halo, inner)])]
    part = project(fixed, middle, [(HB, rows - HB)], groups, last=False)[0]
    rim = jnp.concatenate([low, high, far_low, far_high, far_ends], axis=1)
    rim_other = cores(rim)
    own_rim = [(rim, rim_other, [(0, 0, halo), (halo, halo + inner, halo)])]
    far_rim = [
        (
            rim,
            rim_other,
            [
                (2 * halo, 0, halo),
                (3 * halo, halo + inner, halo),
                (4 * halo, halo, halo),
                (5 * halo, inner, halo),
            ],
        )
    ]
    send_a, keep_a = project(fixed, middle + own_rim, [(0, HB), (rows - HB, rows)], groups, before=part)
    send_a, far_front = lax.optimization_barrier((send_a, far_front))
    got_a = swap(send_a, 1)
    far_middle = [
        (far_front, cores(far_front), [(0, 2 * halo, half - halo)]),
    ]
    send_b, keep_b = project(fixed, far_rim + far_middle, [(0, rows)], groups)
    got_b = swap(send_b, 1)
    keep, *sends = spread(groups, keep_a, got_a, keep_b, got_b)
    return finish(keep, [swap(send, 2 * step) for step, send in enumerate(sends, 1)])


def solution(mesh):
    in_specs = (
        P("node", "col"),
        P("node", "col"),
        P("node", None, None, None),
        P("node", None, None, None),
        P("node", None),
    )
    out_specs = (P(("col", "node"), None), P(("col", "node"), None))
    return jax.shard_map(body, mesh=mesh, in_specs=in_specs, out_specs=out_specs, check_vma=False)
```

```python
import functools

import jax
import jax.numpy as jnp
from jax import lax
from jax.experimental import pallas as pl
from jax.experimental.pallas import tpu as pltpu
from jax.sharding import PartitionSpec as P

BS = 128
HB = 4
ROWS_OF_CORE = 64
FETCHES = 4
MIB = 1024 * 1024
F32 = jnp.float32
BF16 = jnp.bfloat16
VMEM = pl.BlockSpec(memory_space=pltpu.VMEM)
SMEM = pl.BlockSpec(memory_space=pltpu.SMEM)
HBM = pl.BlockSpec(memory_space=pl.ANY)


def params(mib):
    return pltpu.CompilerParams(vmem_limit_bytes=mib * MIB)


def shape(dims, kind):
    return jax.ShapeDtypeStruct(dims, kind)


def cut_kernel(panel, ends, middle, sems):
    inner = panel.shape[1]
    halo = HB * BS
    odd = lax.axis_index("node") % 2
    to_pair = pl.multiple_of((1 - odd) * (inner - halo), BS)
    to_next = pl.multiple_of(odd * (inner - halo), BS)
    copies = [
        (panel.at[:, pl.ds(to_pair, halo)], ends.at[:, 0:halo]),
        (panel.at[:, pl.ds(to_next, halo)], ends.at[:, halo:2 * halo]),
        (panel.at[:, halo:inner - halo], middle),
    ]
    copies = [pltpu.make_async_copy(*pair, sems.at[i]) for i, pair in enumerate(copies)]
    for copy in copies:
        copy.start()
    for copy in copies:
        copy.wait()


def cut(panel):
    width, inner = panel.shape
    halo = HB * BS
    return pl.pallas_call(
        cut_kernel,
        out_shape=[shape((width, w), BF16) for w in (2 * halo, inner - 2 * halo)],
        in_specs=[HBM],
        out_specs=[VMEM] * 2,
        scratch_shapes=[pltpu.SemaphoreType.DMA((3,))],
        compiler_params=params(58),
    )(panel)


def project_kernel(spans, places, groups, more, fetch, *refs):
    ids_ref, g_ref, c_ref, basis_ref = refs[:4]
    pieces = refs[4:4 + 2 * len(places)]
    rest = list(refs[4 + 2 * len(places):])
    before = rest.pop(0) if more else None
    rows, slots = g_ref.shape[0], g_ref.shape[1]
    width = ROWS_OF_CORE
    node = lax.axis_index("node")
    core = lax.axis_index("col") % 2
    odd = node % 2
    arrivals = {}
    sems = rest.pop()
    basis_new = rest.pop()
    if fetch:
        g_new, c_new = rest[1:3]
        del rest[1:3]
        edges = [rows * i // FETCHES for i in range(FETCHES + 1)]
        for step, (lo, hi) in enumerate(zip(edges[:-1], edges[1:])):
            arrivals[lo] = [
                pltpu.make_async_copy(old.at[lo:hi], new.at[lo:hi], sems.at[step, which])
                for which, (old, new) in enumerate(((g_ref, g_new), (c_ref, c_new)))
            ]
        for batch in arrivals.values():
            for copy in batch:
                copy.start()
        g_ref, c_ref = g_new, c_new
    basis_copies = []
    at = 0
    for step, (lo, hi) in enumerate(spans):
        target = basis_new.at[at:at + (hi - lo) * BS]
        basis_copies.append(pltpu.make_async_copy(basis_ref.at[lo * BS:hi * BS], target, sems.at[step, 2]))
        basis_copies[-1].start()
        at += (hi - lo) * BS
    *outs, ext, prods = rest

    for which, (base, parts) in enumerate(places):
        for owner, ref in ((core, pieces[2 * which]), (1 - core, pieces[2 * which + 1])):
            at = pl.ds(pl.multiple_of(owner * width, width), width)
            for source, even_target, odd_target, count in parts:
                target = even_target
                if odd_target != even_target:
                    target = pl.multiple_of(even_target + odd * (odd_target - even_target), BS)
                ext[at, pl.ds(target, count)] = ref[base:base + width, source:source + count]

    offset = node * rows - HB
    at = 0
    total = None
    for step, (lo, hi) in enumerate(spans):
        begin = at
        for row in range(lo, hi):
            for first in [first for first in arrivals if first <= row]:
                for copy in arrivals.pop(first):
                    copy.wait()
            near = []
            for slot in range(slots):
                local = jnp.clip(ids_ref[slot, row] - offset, 0, rows + 2 * HB - 1)
                near.append(ext[:, pl.ds(pl.multiple_of(local * BS, BS), BS)])
            near = jnp.concatenate(near, axis=1)
            both = jnp.concatenate(
                [jnp.concatenate([ref[row, slot] for slot in range(slots)], axis=1) for ref in (g_ref, c_ref)], axis=0
            )
            prod = lax.dot_general(both, near, (((1,), (1,)), ((), ())), preferred_element_type=F32).astype(BF16)
            prods[at:at + BS, 0:2 * width] = prod[0:BS]
            prods[at:at + BS, 2 * width:4 * width] = prod[BS:2 * BS]
            at += BS
        basis_copies[step].wait()
        part = lax.dot_general(
            basis_new[begin:at, :], prods[begin:at, :], (((0,), (0,)), ((), ())), preferred_element_type=F32
        )
        total = part if total is None else total + part
    for batch in arrivals.values():
        for copy in batch:
            copy.wait()
    if before is not None:
        total = total + before[...]
    if len(outs) == 1:
        outs[0][...] = total
        return
    send_ref, keep_ref = outs
    states, columns = total.shape
    total = total.reshape(groups, 2, states // (2 * groups), columns)
    keep_ref[...] = jnp.where(odd == 1, total[:, 1], total[:, 0])
    send_ref[...] = jnp.where(odd == 1, total[:, 0], total[:, 1]).astype(BF16)


def project(fixed, pieces, spans, groups, before=None, first=False):
    ids, g_blocks, c_blocks, basis = fixed
    rows, slots = g_blocks.shape[0], g_blocks.shape[1]
    width = ROWS_OF_CORE
    states = basis.shape[1]
    piece = (groups, states // (2 * groups), 4 * width)
    arrays = [array for mine, other, _, _ in pieces for array in (mine, other)]
    more = [] if before is None else [before]
    count = sum(hi - lo for lo, hi in spans)
    scratch = [
        pltpu.VMEM((2 * width, (rows + 2 * HB) * BS), BF16),
        pltpu.VMEM((count * BS, 4 * width), BF16),
        pltpu.VMEM((count * BS, states), BF16),
        pltpu.SemaphoreType.DMA((FETCHES, 3)),
    ]
    if first:
        outs = [shape((states, 4 * width), F32), shape(g_blocks.shape, BF16), shape(c_blocks.shape, BF16)]
    else:
        outs = [shape(piece, BF16), shape(piece, F32)]
    places = [(base, parts) for _, _, base, parts in pieces]
    return pl.pallas_call(
        functools.partial(project_kernel, spans, places, groups, before is not None, first),
        out_shape=outs,
        in_specs=[SMEM] + [HBM if first else VMEM] * 2 + [HBM] + [VMEM] * (len(arrays) + len(more)),
        out_specs=[VMEM] * len(outs),
        scratch_shapes=scratch,
        compiler_params=params(42),
        cost_estimate=pl.CostEstimate(flops=count, bytes_accessed=count, transcendentals=0),
    )(ids, g_blocks, c_blocks, basis, *arrays, *more)


def spread_kernel(groups, keep_a, got_a, keep_b, got_b, keep_ref, *send_refs):
    here = lax.axis_index("node") // 2
    half = keep_a.shape[2]
    for step in range(groups):
        at = here ^ step
        for lo, keep, got in ((0, keep_a, got_a), (half, keep_b, got_b)):
            value = keep[at] + got[at].astype(F32)
            if step == 0:
                keep_ref[:, lo:lo + half] = value
            else:
                send_refs[step - 1][:, lo:lo + half] = value.astype(BF16)


def spread(groups, keep_a, got_a, keep_b, got_b):
    piece = (keep_a.shape[1], 2 * keep_a.shape[2])
    return pl.pallas_call(
        functools.partial(spread_kernel, groups),
        out_shape=[shape(piece, F32)] + [shape(piece, BF16)] * (groups - 1),
        in_specs=[VMEM] * 4,
        out_specs=[VMEM] * groups,
        compiler_params=params(4),
    )(keep_a, got_a, keep_b, got_b)


def finish_kernel(keep, *refs):
    got, (out_g, out_c) = refs[:-2], refs[-2:]
    total = keep[...]
    for ref in got:
        total = total + ref[...].astype(F32)
    first = lax.axis_index("col") // 2
    quarter = total.shape[1] // 4
    for place, base in ((first, 0), (1 - first, 2 * quarter)):
        at = pl.ds(pl.multiple_of(place * quarter, quarter), quarter)
        out_g[:, at] = total[:, base:base + quarter]
        out_c[:, at] = total[:, base + quarter:base + 2 * quarter]


def finish(keep, got):
    piece = shape((keep.shape[0], keep.shape[1] // 2), F32)
    return pl.pallas_call(
        finish_kernel,
        out_shape=(piece, piece),
        in_specs=[VMEM] * (1 + len(got)),
        out_specs=(VMEM, VMEM),
        compiler_params=params(4),
    )(keep, *got)


def body(panel, basis, g_blocks, c_blocks, block_cols):
    nodes, cols = lax.axis_size("node"), lax.axis_size("col")
    rows = g_blocks.shape[0]
    groups = nodes // 2
    halo = HB * BS
    inner = rows * BS
    ids = block_cols.T
    mine = panel.T

    def across(array):
        return lax.ppermute(array, "col", [(i, i ^ 2) for i in range(cols)])

    def cores(array):
        return lax.ppermute(array, "col", [(i, i ^ 1) for i in range(cols)])

    def swap(array, step):
        return lax.ppermute(array, "node", [(i, i ^ step) for i in range(nodes)])

    def swap_next(array):
        pairs = [(i, i + 1) for i in range(1, nodes - 1, 2)]
        return lax.ppermute(array, "node", pairs + [(j, i) for i, j in pairs])

    other = cores(mine)
    ends, middle = cut(mine)
    far_ends, far_middle = across(ends), across(middle)
    all_ends = jnp.concatenate([ends, far_ends], axis=0)
    rim = jnp.concatenate([swap(all_ends[:, :halo], 1), swap_next(all_ends[:, halo:])], axis=1)
    own = [(mine, other, 0, [(0, halo, halo, inner)])]
    part, g_blocks, c_blocks = project(
        (ids, g_blocks, c_blocks, basis), own, [(HB, rows - HB)], groups, first=True
    )
    part, far_middle = lax.optimization_barrier((part, far_middle))
    fixed = (ids, g_blocks, c_blocks, basis)
    rim_other = cores(rim)
    rim_parts = [(0, halo + inner, 0, halo), (halo, 0, halo + inner, halo)]
    send_a, keep_a = project(
        fixed, own + [(rim, rim_other, 0, rim_parts)], [(0, HB), (rows - HB, rows)], groups, before=part
    )
    got_a = swap(send_a, 1)
    far = [
        (rim, rim_other, ROWS_OF_CORE, rim_parts),
        (far_ends, cores(far_ends), 0, [(0, inner, halo, halo), (halo, halo, inner, halo)]),
        (far_middle, cores(far_middle), 0, [(0, 2 * halo, 2 * halo, inner - 2 * halo)]),
    ]
    send_b, keep_b = project(fixed, far, [(0, rows)], groups)
    got_b = swap(send_b, 1)
    keep, *sends = spread(groups, keep_a, got_a, keep_b, got_b)
    return finish(keep, [swap(send, 2 * step) for step, send in enumerate(sends, 1)])


def solution(mesh):
    in_specs = (
        P("node", "col"),
        P("node", "col"),
        P("node", None, None, None),
        P("node", None, None, None),
        P("node", None),
    )
    out_specs = (P(("col", "node"), None), P(("col", "node"), None))
    return jax.shard_map(body, mesh=mesh, in_specs=in_specs, out_specs=out_specs, check_vma=False)
```

```python
import functools

import jax
import jax.numpy as jnp
from jax import lax
from jax.experimental import pallas as pl
from jax.experimental.pallas import tpu as pltpu
from jax.sharding import PartitionSpec as P

BS = 128
HB = 4
ROWS_OF_CORE = 64
MIB = 1024 * 1024
F32 = jnp.float32
BF16 = jnp.bfloat16
VMEM = pl.BlockSpec(memory_space=pltpu.VMEM)
SMEM = pl.BlockSpec(memory_space=pltpu.SMEM)
HBM = pl.BlockSpec(memory_space=pl.ANY)


def params(mib):
    return pltpu.CompilerParams(vmem_limit_bytes=mib * MIB)


def shape(dims, kind):
    return jax.ShapeDtypeStruct(dims, kind)


def cut_kernel(panel, ends, middle, sems):
    inner = panel.shape[1]
    halo = HB * BS
    odd = lax.axis_index("node") % 2
    to_pair = pl.multiple_of((1 - odd) * (inner - halo), BS)
    to_next = pl.multiple_of(odd * (inner - halo), BS)
    copies = [
        (panel.at[:, pl.ds(to_pair, halo)], ends.at[:, 0:halo]),
        (panel.at[:, pl.ds(to_next, halo)], ends.at[:, halo:2 * halo]),
        (panel.at[:, halo:inner - halo], middle),
    ]
    copies = [pltpu.make_async_copy(*pair, sems.at[i]) for i, pair in enumerate(copies)]
    for copy in copies:
        copy.start()
    for copy in copies:
        copy.wait()


def cut(panel):
    width, inner = panel.shape
    halo = HB * BS
    return pl.pallas_call(
        cut_kernel,
        out_shape=[shape((width, w), BF16) for w in (2 * halo, inner - 2 * halo)],
        in_specs=[HBM],
        out_specs=[VMEM] * 2,
        scratch_shapes=[pltpu.SemaphoreType.DMA((3,))],
        compiler_params=params(44),
    )(panel)


def load_kernel(*refs):
    count = len(refs) // 2
    sources, targets, sems = refs[:count], refs[count:2 * count], refs[-1]
    copies = []
    for which, (source, target) in enumerate(zip(sources, targets)):
        middle = source.shape[0] // 2
        for part, span in enumerate((pl.ds(0, middle), pl.ds(middle, source.shape[0] - middle))):
            copies.append(pltpu.make_async_copy(source.at[span], target.at[span], sems.at[which, part]))
    for copy in copies:
        copy.start()
    for copy in copies:
        copy.wait()


def load(*arrays):
    size = sum(array.size * array.dtype.itemsize for array in arrays)
    return pl.pallas_call(
        load_kernel,
        out_shape=[shape(array.shape, array.dtype) for array in arrays],
        in_specs=[HBM] * len(arrays),
        out_specs=[VMEM] * len(arrays),
        scratch_shapes=[pltpu.SemaphoreType.DMA((len(arrays), 2))],
        compiler_params=params(45),
        cost_estimate=pl.CostEstimate(flops=0, bytes_accessed=size, transcendentals=0),
    )(*arrays)


def project_kernel(spans, places, groups, more, *refs):
    ids_ref, g_ref, c_ref, basis_ref = refs[:4]
    pieces = refs[4:4 + 2 * len(places)]
    rest = list(refs[4 + 2 * len(places):])
    before = rest.pop(0) if more else None
    *outs, ext, prods = rest
    slots = g_ref.shape[1]
    width = ROWS_OF_CORE
    core = lax.axis_index("col") % 2
    odd = lax.axis_index("node") % 2

    for which, (base, parts) in enumerate(places):
        for owner, ref in ((core, pieces[2 * which]), (1 - core, pieces[2 * which + 1])):
            at = pl.ds(pl.multiple_of(owner * width, width), width)
            for source, even_target, odd_target, count in parts:
                target = even_target
                if odd_target != even_target:
                    target = pl.multiple_of(even_target + odd * (odd_target - even_target), BS)
                ext[at, pl.ds(target, count)] = ref[base:base + width, source:source + count]

    at = 0
    total = None
    for lo, hi in spans:
        begin = at
        for row in range(lo, hi):
            near = jnp.concatenate(
                [ext[:, pl.ds(pl.multiple_of(ids_ref[slot, row] * BS, BS), BS)] for slot in range(slots)], axis=1
            )
            both = jnp.concatenate(
                [jnp.concatenate([ref[row, slot] for slot in range(slots)], axis=1) for ref in (g_ref, c_ref)], axis=0
            )
            prod = lax.dot_general(both, near, (((1,), (1,)), ((), ())), preferred_element_type=F32).astype(BF16)
            prods[at:at + BS, 0:2 * width] = prod[0:BS]
            prods[at:at + BS, 2 * width:4 * width] = prod[BS:2 * BS]
            at += BS
        part = lax.dot_general(
            basis_ref[lo * BS:hi * BS, :], prods[begin:at, :], (((0,), (0,)), ((), ())), preferred_element_type=F32
        )
        total = part if total is None else total + part
    if before is not None:
        total = total + before[...]
    if len(outs) == 1:
        outs[0][...] = total
        return
    send_ref, keep_ref = outs
    states, columns = total.shape
    total = total.reshape(groups, 2, states // (2 * groups), columns)
    keep_ref[...] = jnp.where(odd == 1, total[:, 1], total[:, 0])
    send_ref[...] = jnp.where(odd == 1, total[:, 0], total[:, 1]).astype(BF16)


def project(fixed, pieces, spans, groups, before=None, last=True):
    ids, g_blocks, c_blocks, basis = fixed
    rows, slots = g_blocks.shape[0], g_blocks.shape[1]
    width = ROWS_OF_CORE
    states = basis.shape[1]
    piece = (groups, states // (2 * groups), 4 * width)
    arrays = [array for mine, other, _, _ in pieces for array in (mine, other)]
    more = [] if before is None else [before]
    count = sum(hi - lo for lo, hi in spans)
    outs = [shape(piece, BF16), shape(piece, F32)] if last else [shape((states, 4 * width), F32)]
    places = [(base, parts) for _, _, base, parts in pieces]
    return pl.pallas_call(
        functools.partial(project_kernel, spans, places, groups, before is not None),
        out_shape=outs,
        in_specs=[SMEM] + [VMEM] * (3 + len(arrays) + len(more)),
        out_specs=[VMEM] * len(outs),
        scratch_shapes=[
            pltpu.VMEM((2 * width, (rows + 2 * HB) * BS), BF16),
            pltpu.VMEM((count * BS, 4 * width), BF16),
        ],
        compiler_params=params(14),
        cost_estimate=pl.CostEstimate(flops=count, bytes_accessed=count, transcendentals=0),
    )(ids, g_blocks, c_blocks, basis, *arrays, *more)


def spread_kernel(groups, keep_a, got_a, keep_b, got_b, keep_ref, *send_refs):
    here = lax.axis_index("node") // 2
    half = keep_a.shape[2]
    for step in range(groups):
        at = here ^ step
        for lo, keep, got in ((0, keep_a, got_a), (half, keep_b, got_b)):
            value = keep[at] + got[at].astype(F32)
            if step == 0:
                keep_ref[:, lo:lo + half] = value
            else:
                send_refs[step - 1][:, lo:lo + half] = value.astype(BF16)


def spread(groups, keep_a, got_a, keep_b, got_b):
    piece = (keep_a.shape[1], 2 * keep_a.shape[2])
    return pl.pallas_call(
        functools.partial(spread_kernel, groups),
        out_shape=[shape(piece, F32)] + [shape(piece, BF16)] * (groups - 1),
        in_specs=[VMEM] * 4,
        out_specs=[VMEM] * groups,
        compiler_params=params(4),
    )(keep_a, got_a, keep_b, got_b)


def finish_kernel(keep, *refs):
    got, (out_g, out_c) = refs[:-2], refs[-2:]
    total = keep[...]
    for ref in got:
        total = total + ref[...].astype(F32)
    first = lax.axis_index("col") // 2
    quarter = total.shape[1] // 4
    for place, base in ((first, 0), (1 - first, 2 * quarter)):
        at = pl.ds(pl.multiple_of(place * quarter, quarter), quarter)
        out_g[:, at] = total[:, base:base + quarter]
        out_c[:, at] = total[:, base + quarter:base + 2 * quarter]


def finish(keep, got):
    piece = shape((keep.shape[0], keep.shape[1] // 2), F32)
    return pl.pallas_call(
        finish_kernel,
        out_shape=(piece, piece),
        in_specs=[VMEM] * (1 + len(got)),
        out_specs=(VMEM, VMEM),
        compiler_params=params(4),
    )(keep, *got)


def body(panel, basis, g_blocks, c_blocks, block_cols):
    nodes, cols = lax.axis_size("node"), lax.axis_size("col")
    rows = g_blocks.shape[0]
    groups = nodes // 2
    halo = HB * BS
    inner = rows * BS

    def across(array):
        return lax.ppermute(array, "col", [(i, i ^ 2) for i in range(cols)])

    def cores(array):
        return lax.ppermute(array, "col", [(i, i ^ 1) for i in range(cols)])

    def swap(array, step):
        return lax.ppermute(array, "node", [(i, i ^ step) for i in range(nodes)])

    def swap_next(array):
        pairs = [(i, i + 1) for i in range(1, nodes - 1, 2)]
        return lax.ppermute(array, "node", pairs + [(j, i) for i, j in pairs])

    ends, middle = cut(panel.T)
    far_ends, far_middle = across(ends), across(middle)
    own = [
        (ends, cores(ends), 0, [(0, inner, halo, halo), (halo, halo, inner, halo)]),
        (middle, cores(middle), 0, [(0, 2 * halo, 2 * halo, inner - 2 * halo)]),
    ]
    g_blocks, c_blocks = load(g_blocks, c_blocks)
    (basis,) = load(basis)
    ids = jnp.clip(block_cols.T - (lax.axis_index("node") * rows - HB), 0, rows + 2 * HB - 1)
    far_ends, g_blocks, c_blocks, basis, ids = lax.optimization_barrier((far_ends, g_blocks, c_blocks, basis, ids))
    all_ends = jnp.concatenate([ends, far_ends], axis=0)
    rim = jnp.concatenate([swap(all_ends[:, :halo], 1), swap_next(all_ends[:, halo:])], axis=1)
    fixed = (ids, g_blocks, c_blocks, basis)
    (part,) = project(fixed, own, [(HB, rows - HB)], groups, last=False)
    part, far_middle = lax.optimization_barrier((part, far_middle))
    rim_other = cores(rim)
    rim_parts = [(0, halo + inner, 0, halo), (halo, 0, halo + inner, halo)]
    send_a, keep_a = project(
        fixed, own + [(rim, rim_other, 0, rim_parts)], [(0, HB), (rows - HB, rows)], groups, before=part
    )
    got_a = swap(send_a, 1)
    far = [
        (rim, rim_other, ROWS_OF_CORE, rim_parts),
        (far_ends, cores(far_ends), 0, [(0, inner, halo, halo), (halo, halo, inner, halo)]),
        (far_middle, cores(far_middle), 0, [(0, 2 * halo, 2 * halo, inner - 2 * halo)]),
    ]
    send_b, keep_b = project(fixed, far, [(0, rows)], groups)
    got_b = swap(send_b, 1)
    keep, *sends = spread(groups, keep_a, got_a, keep_b, got_b)
    return finish(keep, [swap(send, 2 * step) for step, send in enumerate(sends, 1)])


def solution(mesh):
    in_specs = (
        P("node", "col"),
        P("node", "col"),
        P("node", None, None, None),
        P("node", None, None, None),
        P("node", None),
    )
    out_specs = (P(("col", "node"), None), P(("col", "node"), None))
    return jax.shard_map(body, mesh=mesh, in_specs=in_specs, out_specs=out_specs, check_vma=False)
```

```python
import functools

import jax
import jax.numpy as jnp
from jax import lax
from jax.experimental import pallas as pl
from jax.experimental.pallas import tpu as pltpu
from jax.sharding import PartitionSpec as P

BS = 128
HB = 4
ROWS_OF_CORE = 64
MIB = 1024 * 1024
F32 = jnp.float32
BF16 = jnp.bfloat16
VMEM = pl.BlockSpec(memory_space=pltpu.VMEM)
SMEM = pl.BlockSpec(memory_space=pltpu.SMEM)
HBM = pl.BlockSpec(memory_space=pl.ANY)


def params(mib):
    return pltpu.CompilerParams(vmem_limit_bytes=mib * MIB)


def shape(dims, kind):
    return jax.ShapeDtypeStruct(dims, kind)


def cut_kernel(panel, ends, middle, sems):
    inner = panel.shape[1]
    halo = HB * BS
    odd = lax.axis_index("node") % 2
    to_pair = pl.multiple_of((1 - odd) * (inner - halo), BS)
    to_next = pl.multiple_of(odd * (inner - halo), BS)
    copies = [
        (panel.at[:, pl.ds(to_pair, halo)], ends.at[:, 0:halo]),
        (panel.at[:, pl.ds(to_next, halo)], ends.at[:, halo:2 * halo]),
        (panel.at[:, halo:inner - halo], middle),
    ]
    copies = [pltpu.make_async_copy(*pair, sems.at[i]) for i, pair in enumerate(copies)]
    for copy in copies:
        copy.start()
    for copy in copies:
        copy.wait()


def cut(panel):
    width, inner = panel.shape
    halo = HB * BS
    return pl.pallas_call(
        cut_kernel,
        out_shape=[shape((width, w), BF16) for w in (2 * halo, inner - 2 * halo)],
        in_specs=[HBM],
        out_specs=[VMEM] * 2,
        scratch_shapes=[pltpu.SemaphoreType.DMA((3,))],
        compiler_params=params(44),
    )(panel)


def load_kernel(*refs):
    count = len(refs) // 2
    sources, targets, sems = refs[:count], refs[count:2 * count], refs[-1]
    copies = []
    for which, (source, target) in enumerate(zip(sources, targets)):
        middle = source.shape[0] // 2
        for part, span in enumerate((pl.ds(0, middle), pl.ds(middle, source.shape[0] - middle))):
            copies.append(pltpu.make_async_copy(source.at[span], target.at[span], sems.at[which, part]))
    for copy in copies:
        copy.start()
    for copy in copies:
        copy.wait()


def load(*arrays):
    size = sum(array.size * array.dtype.itemsize for array in arrays)
    return pl.pallas_call(
        load_kernel,
        out_shape=[shape(array.shape, array.dtype) for array in arrays],
        in_specs=[HBM] * len(arrays),
        out_specs=[VMEM] * len(arrays),
        scratch_shapes=[pltpu.SemaphoreType.DMA((len(arrays), 2))],
        compiler_params=params(45),
        cost_estimate=pl.CostEstimate(flops=0, bytes_accessed=size, transcendentals=0),
    )(*arrays)


def project_kernel(spans, places, groups, more, *refs):
    ids_ref, g_ref, c_ref, basis_ref = refs[:4]
    pieces = refs[4:4 + 2 * len(places)]
    rest = list(refs[4 + 2 * len(places):])
    before = rest.pop(0) if more else None
    *outs, ext, prods = rest
    slots = g_ref.shape[1]
    width = ROWS_OF_CORE
    core = lax.axis_index("col") % 2
    odd = lax.axis_index("node") % 2

    for which, (base, parts) in enumerate(places):
        for owner, ref in ((core, pieces[2 * which]), (1 - core, pieces[2 * which + 1])):
            at = pl.ds(pl.multiple_of(owner * width, width), width)
            for source, even_target, odd_target, count in parts:
                target = even_target
                if odd_target != even_target:
                    target = pl.multiple_of(even_target + odd * (odd_target - even_target), BS)
                ext[at, pl.ds(target, count)] = ref[base:base + width, source:source + count]

    at = 0
    total = None
    for lo, hi in spans:
        begin = at
        for row in range(lo, hi):
            near = jnp.concatenate(
                [ext[:, pl.ds(pl.multiple_of(ids_ref[slot, row] * BS, BS), BS)] for slot in range(slots)], axis=1
            )
            both = jnp.concatenate(
                [jnp.concatenate([ref[row, slot] for slot in range(slots)], axis=1) for ref in (g_ref, c_ref)], axis=0
            )
            prod = lax.dot_general(both, near, (((1,), (1,)), ((), ())), preferred_element_type=F32).astype(BF16)
            prods[at:at + BS, 0:2 * width] = prod[0:BS]
            prods[at:at + BS, 2 * width:4 * width] = prod[BS:2 * BS]
            at += BS
        part = lax.dot_general(
            basis_ref[lo * BS:hi * BS, :], prods[begin:at, :], (((0,), (0,)), ((), ())), preferred_element_type=F32
        )
        total = part if total is None else total + part
    if before is not None:
        total = total + before[...]
    if len(outs) == 1:
        outs[0][...] = total
        return
    send_ref, keep_ref = outs
    states, columns = total.shape
    total = total.reshape(groups, 2, states // (2 * groups), columns)
    keep_ref[...] = jnp.where(odd == 1, total[:, 1], total[:, 0])
    send_ref[...] = jnp.where(odd == 1, total[:, 0], total[:, 1]).astype(BF16)


def project(fixed, pieces, spans, groups, before=None, last=True):
    ids, g_blocks, c_blocks, basis = fixed
    rows, slots = g_blocks.shape[0], g_blocks.shape[1]
    width = ROWS_OF_CORE
    states = basis.shape[1]
    piece = (groups, states // (2 * groups), 4 * width)
    arrays = [array for mine, other, _, _ in pieces for array in (mine, other)]
    more = [] if before is None else [before]
    count = sum(hi - lo for lo, hi in spans)
    outs = [shape(piece, BF16), shape(piece, F32)] if last else [shape((states, 4 * width), F32)]
    places = [(base, parts) for _, _, base, parts in pieces]
    return pl.pallas_call(
        functools.partial(project_kernel, spans, places, groups, before is not None),
        out_shape=outs,
        in_specs=[SMEM] + [VMEM] * (3 + len(arrays) + len(more)),
        out_specs=[VMEM] * len(outs),
        scratch_shapes=[
            pltpu.VMEM((2 * width, (rows + 2 * HB) * BS), BF16),
            pltpu.VMEM((count * BS, 4 * width), BF16),
        ],
        compiler_params=params(14),
        cost_estimate=pl.CostEstimate(flops=count, bytes_accessed=count, transcendentals=0),
    )(ids, g_blocks, c_blocks, basis, *arrays, *more)


def spread_kernel(groups, keep, got, keep_ref, *send_refs):
    here = lax.axis_index("node") // 2
    for step in range(groups):
        value = keep[here ^ step] + got[here ^ step].astype(F32)
        if step == 0:
            keep_ref[...] = value
        else:
            send_refs[step - 1][...] = value.astype(BF16)


def spread(groups, keep, got):
    piece = keep.shape[1:]
    return pl.pallas_call(
        functools.partial(spread_kernel, groups),
        out_shape=[shape(piece, F32)] + [shape(piece, BF16)] * (groups - 1),
        in_specs=[VMEM] * 2,
        out_specs=[VMEM] * groups,
        compiler_params=params(4),
    )(keep, got)


def finish_kernel(count, *refs):
    out_g, out_c = refs[-2:]
    quarter = out_g.shape[1] // 2
    first = lax.axis_index("col") // 2
    for place, half in ((first, refs[:count]), (1 - first, refs[count:2 * count])):
        total = half[0][...]
        for ref in half[1:]:
            total = total + ref[...].astype(F32)
        at = pl.ds(pl.multiple_of(place * quarter, quarter), quarter)
        out_g[:, at] = total[:, 0:quarter]
        out_c[:, at] = total[:, quarter:2 * quarter]


def finish(own, far):
    piece = shape(own[0].shape, F32)
    return pl.pallas_call(
        functools.partial(finish_kernel, len(own)),
        out_shape=(piece, piece),
        in_specs=[VMEM] * (len(own) + len(far)),
        out_specs=(VMEM, VMEM),
        compiler_params=params(4),
    )(*own, *far)


def body(panel, basis, g_blocks, c_blocks, block_cols):
    nodes, cols = lax.axis_size("node"), lax.axis_size("col")
    rows = g_blocks.shape[0]
    groups = nodes // 2
    halo = HB * BS
    inner = rows * BS

    def across(array):
        return lax.ppermute(array, "col", [(i, i ^ 2) for i in range(cols)])

    def cores(array):
        return lax.ppermute(array, "col", [(i, i ^ 1) for i in range(cols)])

    def swap(array, step):
        return lax.ppermute(array, "node", [(i, i ^ step) for i in range(nodes)])

    def swap_next(array):
        pairs = [(i, i + 1) for i in range(1, nodes - 1, 2)]
        return lax.ppermute(array, "node", pairs + [(j, i) for i, j in pairs])

    ends, middle = cut(panel.T)
    far_ends, far_middle = across(ends), across(middle)
    own = [
        (ends, cores(ends), 0, [(0, inner, halo, halo), (halo, halo, inner, halo)]),
        (middle, cores(middle), 0, [(0, 2 * halo, 2 * halo, inner - 2 * halo)]),
    ]
    g_blocks, c_blocks = load(g_blocks, c_blocks)
    (basis,) = load(basis)
    ids = jnp.clip(block_cols.T - (lax.axis_index("node") * rows - HB), 0, rows + 2 * HB - 1)
    far_ends, g_blocks, c_blocks, basis, ids = lax.optimization_barrier((far_ends, g_blocks, c_blocks, basis, ids))
    all_ends = jnp.concatenate([ends, far_ends], axis=0)
    rim = jnp.concatenate([swap(all_ends[:, :halo], 1), swap_next(all_ends[:, halo:])], axis=1)
    fixed = (ids, g_blocks, c_blocks, basis)
    (part,) = project(fixed, own, [(HB, rows - HB)], groups, last=False)
    part, far_middle = lax.optimization_barrier((part, far_middle))
    rim_other = cores(rim)
    rim_parts = [(0, halo + inner, 0, halo), (halo, 0, halo + inner, halo)]
    send_a, keep_a = project(
        fixed, own + [(rim, rim_other, 0, rim_parts)], [(0, HB), (rows - HB, rows)], groups, before=part
    )
    got_a = swap(send_a, 1)
    far = [
        (rim, rim_other, ROWS_OF_CORE, rim_parts),
        (far_ends, cores(far_ends), 0, [(0, inner, halo, halo), (halo, halo, inner, halo)]),
        (far_middle, cores(far_middle), 0, [(0, 2 * halo, 2 * halo, inner - 2 * halo)]),
    ]
    send_b, keep_b = project(fixed, far, [(0, rows)], groups)
    got_b = swap(send_b, 1)
    halves = []
    for keep, got in ((keep_a, got_a), (keep_b, got_b)):
        keep, *sends = spread(groups, keep, got)
        halves.append([keep] + [swap(send, 2 * step) for step, send in enumerate(sends, 1)])
    return finish(*halves)


def solution(mesh):
    in_specs = (
        P("node", "col"),
        P("node", "col"),
        P("node", None, None, None),
        P("node", None, None, None),
        P("node", None),
    )
    out_specs = (P(("col", "node"), None), P(("col", "node"), None))
    return jax.shard_map(body, mesh=mesh, in_specs=in_specs, out_specs=out_specs, check_vma=False)
```

```python
import functools

import jax
import jax.numpy as jnp
from jax import lax
from jax.experimental import pallas as pl
from jax.experimental.pallas import tpu as pltpu
from jax.sharding import PartitionSpec as P

BS = 128
HB = 4
ROWS_OF_CORE = 64
MIB = 1024 * 1024
F32 = jnp.float32
BF16 = jnp.bfloat16
VMEM = pl.BlockSpec(memory_space=pltpu.VMEM)
SMEM = pl.BlockSpec(memory_space=pltpu.SMEM)
HBM = pl.BlockSpec(memory_space=pl.ANY)


def params(mib):
    return pltpu.CompilerParams(vmem_limit_bytes=mib * MIB)


def shape(dims, kind):
    return jax.ShapeDtypeStruct(dims, kind)


def cut_kernel(panel, ends, middle, sems):
    inner = panel.shape[1]
    halo = HB * BS
    odd = lax.axis_index("node") % 2
    to_pair = pl.multiple_of((1 - odd) * (inner - halo), BS)
    to_next = pl.multiple_of(odd * (inner - halo), BS)
    copies = [
        (panel.at[:, pl.ds(to_pair, halo)], ends.at[:, 0:halo]),
        (panel.at[:, pl.ds(to_next, halo)], ends.at[:, halo:2 * halo]),
        (panel.at[:, halo:inner - halo], middle),
    ]
    copies = [pltpu.make_async_copy(*pair, sems.at[i]) for i, pair in enumerate(copies)]
    for copy in copies:
        copy.start()
    for copy in copies:
        copy.wait()


def cut(panel):
    width, inner = panel.shape
    halo = HB * BS
    return pl.pallas_call(
        cut_kernel,
        out_shape=[shape((width, w), BF16) for w in (2 * halo, inner - 2 * halo)],
        in_specs=[HBM],
        out_specs=[VMEM] * 2,
        scratch_shapes=[pltpu.SemaphoreType.DMA((3,))],
        compiler_params=params(44),
    )(panel)


def load_kernel(*refs):
    count = len(refs) // 2
    sources, targets, sems = refs[:count], refs[count:2 * count], refs[-1]
    copies = []
    for which, (source, target) in enumerate(zip(sources, targets)):
        middle = source.shape[0] // 2
        for part, span in enumerate((pl.ds(0, middle), pl.ds(middle, source.shape[0] - middle))):
            copies.append(pltpu.make_async_copy(source.at[span], target.at[span], sems.at[which, part]))
    for copy in copies:
        copy.start()
    for copy in copies:
        copy.wait()


def load(*arrays):
    size = sum(array.size * array.dtype.itemsize for array in arrays)
    return pl.pallas_call(
        load_kernel,
        out_shape=[shape(array.shape, array.dtype) for array in arrays],
        in_specs=[HBM] * len(arrays),
        out_specs=[VMEM] * len(arrays),
        scratch_shapes=[pltpu.SemaphoreType.DMA((len(arrays), 2))],
        compiler_params=params(45),
        cost_estimate=pl.CostEstimate(flops=0, bytes_accessed=size, transcendentals=0),
    )(*arrays)


def project_kernel(spans, places, groups, more, *refs):
    ids_ref, g_ref, c_ref, basis_ref = refs[:4]
    pieces = refs[4:4 + 2 * len(places)]
    rest = list(refs[4 + 2 * len(places):])
    before = rest.pop(0) if more else None
    *outs, ext, prods = rest
    slots = g_ref.shape[1]
    width = ROWS_OF_CORE
    core = lax.axis_index("col") % 2
    odd = lax.axis_index("node") % 2

    for which, (base, parts) in enumerate(places):
        for owner, ref in ((core, pieces[2 * which]), (1 - core, pieces[2 * which + 1])):
            at = pl.ds(pl.multiple_of(owner * width, width), width)
            for source, even_target, odd_target, count in parts:
                target = even_target
                if odd_target != even_target:
                    target = pl.multiple_of(even_target + odd * (odd_target - even_target), BS)
                ext[at, pl.ds(target, count)] = ref[base:base + width, source:source + count]

    at = 0
    total = None
    for lo, hi in spans:
        begin = at
        for row in range(lo, hi):
            near = jnp.concatenate(
                [ext[:, pl.ds(pl.multiple_of(ids_ref[slot, row] * BS, BS), BS)] for slot in range(slots)], axis=1
            )
            both = jnp.concatenate(
                [jnp.concatenate([ref[row, slot] for slot in range(slots)], axis=1) for ref in (g_ref, c_ref)], axis=0
            )
            prod = lax.dot_general(both, near, (((1,), (1,)), ((), ())), preferred_element_type=F32).astype(BF16)
            prods[at:at + BS, 0:2 * width] = prod[0:BS]
            prods[at:at + BS, 2 * width:4 * width] = prod[BS:2 * BS]
            at += BS
        part = lax.dot_general(
            basis_ref[lo * BS:hi * BS, :], prods[begin:at, :], (((0,), (0,)), ((), ())), preferred_element_type=F32
        )
        total = part if total is None else total + part
    if before is not None:
        total = total + before[...]
    if len(outs) == 1:
        outs[0][...] = total
        return
    send_ref, keep_ref = outs
    states, columns = total.shape
    total = total.reshape(groups, 2, states // (2 * groups), columns)
    keep_ref[...] = jnp.where(odd == 1, total[:, 1], total[:, 0])
    send_ref[...] = jnp.where(odd == 1, total[:, 0], total[:, 1]).astype(BF16)


def project(fixed, pieces, spans, groups, before=None, last=True):
    ids, g_blocks, c_blocks, basis = fixed
    rows, slots = g_blocks.shape[0], g_blocks.shape[1]
    width = ROWS_OF_CORE
    states = basis.shape[1]
    piece = (groups, states // (2 * groups), 4 * width)
    arrays = [array for mine, other, _, _ in pieces for array in (mine, other)]
    more = [] if before is None else [before]
    count = sum(hi - lo for lo, hi in spans)
    outs = [shape(piece, BF16), shape(piece, F32)] if last else [shape((states, 4 * width), F32)]
    places = [(base, parts) for _, _, base, parts in pieces]
    return pl.pallas_call(
        functools.partial(project_kernel, spans, places, groups, before is not None),
        out_shape=outs,
        in_specs=[SMEM] + [VMEM] * (3 + len(arrays) + len(more)),
        out_specs=[VMEM] * len(outs),
        scratch_shapes=[
            pltpu.VMEM((2 * width, (rows + 2 * HB) * BS), BF16),
            pltpu.VMEM((count * BS, 4 * width), BF16),
        ],
        compiler_params=params(14),
        cost_estimate=pl.CostEstimate(flops=count, bytes_accessed=count, transcendentals=0),
    )(ids, g_blocks, c_blocks, basis, *arrays, *more)


def spread_kernel(groups, keep, got, keep_ref, *send_refs):
    here = lax.axis_index("node") // 2
    for step in range(groups):
        value = keep[here ^ step] + got[here ^ step].astype(F32)
        if step == 0:
            keep_ref[...] = value
        else:
            send_refs[step - 1][...] = value.astype(BF16)


def spread(groups, keep, got):
    piece = keep.shape[1:]
    return pl.pallas_call(
        functools.partial(spread_kernel, groups),
        out_shape=[shape(piece, F32)] + [shape(piece, BF16)] * (groups - 1),
        in_specs=[VMEM] * 2,
        out_specs=[VMEM] * groups,
        compiler_params=params(4),
    )(keep, got)


def finish_kernel(count, *refs):
    out_g, out_c = refs[-2:]
    quarter = out_g.shape[1] // 2
    first = lax.axis_index("col") // 2
    for place, half in ((first, refs[:count]), (1 - first, refs[count:2 * count])):
        total = half[0][...]
        for ref in half[1:]:
            total = total + ref[...].astype(F32)
        at = pl.ds(pl.multiple_of(place * quarter, quarter), quarter)
        out_g[:, at] = total[:, 0:quarter]
        out_c[:, at] = total[:, quarter:2 * quarter]


def finish(own, far):
    piece = shape(own[0].shape, F32)
    return pl.pallas_call(
        functools.partial(finish_kernel, len(own)),
        out_shape=(piece, piece),
        in_specs=[VMEM] * (len(own) + len(far)),
        out_specs=(VMEM, VMEM),
        compiler_params=params(4),
    )(*own, *far)


def body(panel, basis, g_blocks, c_blocks, block_cols):
    nodes, cols = lax.axis_size("node"), lax.axis_size("col")
    rows = g_blocks.shape[0]
    groups = nodes // 2
    halo = HB * BS
    inner = rows * BS

    def across(array):
        return lax.ppermute(array, "col", [(i, i ^ 2) for i in range(cols)])

    def cores(array):
        return lax.ppermute(array, "col", [(i, i ^ 1) for i in range(cols)])

    def swap(array, step):
        return lax.ppermute(array, "node", [(i, i ^ step) for i in range(nodes)])

    def swap_next(array):
        pairs = [(i, i + 1) for i in range(1, nodes - 1, 2)]
        return lax.ppermute(array, "node", pairs + [(j, i) for i, j in pairs])

    ends, middle = cut(panel.T)
    far_ends, far_middle = across(ends), across(middle)
    own = [
        (ends, cores(ends), 0, [(0, inner, halo, halo), (halo, halo, inner, halo)]),
        (middle, cores(middle), 0, [(0, 2 * halo, 2 * halo, inner - 2 * halo)]),
    ]
    g_blocks, c_blocks = load(g_blocks, c_blocks)
    (basis,) = load(basis)
    ids = jnp.clip(block_cols.T - (lax.axis_index("node") * rows - HB), 0, rows + 2 * HB - 1)
    far_ends, basis, ids = lax.optimization_barrier((far_ends, basis, ids))
    all_ends = jnp.concatenate([ends, far_ends], axis=0)
    rim = jnp.concatenate([swap(all_ends[:, :halo], 1), swap_next(all_ends[:, halo:])], axis=1)
    fixed = (ids, g_blocks, c_blocks, basis)
    (part,) = project(fixed, own, [(HB, rows - HB)], groups, last=False)
    part, far_middle = lax.optimization_barrier((part, far_middle))
    rim_other = cores(rim)
    rim_parts = [(0, halo + inner, 0, halo), (halo, 0, halo + inner, halo)]
    send_a, keep_a = project(
        fixed, own + [(rim, rim_other, 0, rim_parts)], [(0, HB), (rows - HB, rows)], groups, before=part
    )
    got_a = swap(send_a, 1)
    far = [
        (rim, rim_other, ROWS_OF_CORE, rim_parts),
        (far_ends, cores(far_ends), 0, [(0, inner, halo, halo), (halo, halo, inner, halo)]),
        (far_middle, cores(far_middle), 0, [(0, 2 * halo, 2 * halo, inner - 2 * halo)]),
    ]
    send_b, keep_b = project(fixed, far, [(0, rows)], groups)
    got_b = swap(send_b, 1)
    halves = []
    for keep, got in ((keep_a, got_a), (keep_b, got_b)):
        keep, *sends = spread(groups, keep, got)
        halves.append([keep] + [swap(send, 2 * step) for step, send in enumerate(sends, 1)])
    return finish(*halves)


def solution(mesh):
    in_specs = (
        P("node", "col"),
        P("node", "col"),
        P("node", None, None, None),
        P("node", None, None, None),
        P("node", None),
    )
    out_specs = (P(("col", "node"), None), P(("col", "node"), None))
    return jax.shard_map(body, mesh=mesh, in_specs=in_specs, out_specs=out_specs, check_vma=False)
```

```python
import functools

import jax
import jax.numpy as jnp
from jax import lax
from jax.experimental import pallas as pl
from jax.experimental.pallas import tpu as pltpu
from jax.sharding import PartitionSpec as P

BS = 128
HB = 4
ROWS_OF_CORE = 64
MIB = 1024 * 1024
F32 = jnp.float32
BF16 = jnp.bfloat16
VMEM = pl.BlockSpec(memory_space=pltpu.VMEM)
SMEM = pl.BlockSpec(memory_space=pltpu.SMEM)
HBM = pl.BlockSpec(memory_space=pl.ANY)


def params(mib):
    return pltpu.CompilerParams(vmem_limit_bytes=mib * MIB)


def shape(dims, kind):
    return jax.ShapeDtypeStruct(dims, kind)


def cut_kernel(panel, ends, middle, sems):
    inner = panel.shape[1]
    halo = HB * BS
    odd = lax.axis_index("node") % 2
    to_pair = pl.multiple_of((1 - odd) * (inner - halo), BS)
    to_next = pl.multiple_of(odd * (inner - halo), BS)
    copies = [
        (panel.at[:, pl.ds(to_pair, halo)], ends.at[:, 0:halo]),
        (panel.at[:, pl.ds(to_next, halo)], ends.at[:, halo:2 * halo]),
        (panel.at[:, halo:inner - halo], middle),
    ]
    copies = [pltpu.make_async_copy(*pair, sems.at[i]) for i, pair in enumerate(copies)]
    for copy in copies:
        copy.start()
    for copy in copies:
        copy.wait()


def cut(panel):
    width, inner = panel.shape
    halo = HB * BS
    return pl.pallas_call(
        cut_kernel,
        out_shape=[shape((width, w), BF16) for w in (2 * halo, inner - 2 * halo)],
        in_specs=[HBM],
        out_specs=[VMEM] * 2,
        scratch_shapes=[pltpu.SemaphoreType.DMA((3,))],
        compiler_params=params(44),
    )(panel)


def load_kernel(*refs):
    count = len(refs) // 2
    sources, targets, sems = refs[:count], refs[count:2 * count], refs[-1]
    copies = []
    for which, (source, target) in enumerate(zip(sources, targets)):
        middle = source.shape[0] // 2
        for part, span in enumerate((pl.ds(0, middle), pl.ds(middle, source.shape[0] - middle))):
            copies.append(pltpu.make_async_copy(source.at[span], target.at[span], sems.at[which, part]))
    for copy in copies:
        copy.start()
    for copy in copies:
        copy.wait()


def load(*arrays):
    size = sum(array.size * array.dtype.itemsize for array in arrays)
    return pl.pallas_call(
        load_kernel,
        out_shape=[shape(array.shape, array.dtype) for array in arrays],
        in_specs=[HBM] * len(arrays),
        out_specs=[VMEM] * len(arrays),
        scratch_shapes=[pltpu.SemaphoreType.DMA((len(arrays), 2))],
        compiler_params=params(45),
        cost_estimate=pl.CostEstimate(flops=1 * 10**10, bytes_accessed=size, transcendentals=0),
    )(*arrays)


def project_kernel(spans, places, groups, more, *refs):
    ids_ref, g_ref, c_ref, basis_ref = refs[:4]
    pieces = refs[4:4 + 2 * len(places)]
    rest = list(refs[4 + 2 * len(places):])
    before = rest.pop(0) if more else None
    *outs, ext, prods = rest
    slots = g_ref.shape[1]
    width = ROWS_OF_CORE
    core = lax.axis_index("col") % 2
    odd = lax.axis_index("node") % 2

    for which, (base, parts) in enumerate(places):
        for owner, ref in ((core, pieces[2 * which]), (1 - core, pieces[2 * which + 1])):
            at = pl.ds(pl.multiple_of(owner * width, width), width)
            for source, even_target, odd_target, count in parts:
                target = even_target
                if odd_target != even_target:
                    target = pl.multiple_of(even_target + odd * (odd_target - even_target), BS)
                ext[at, pl.ds(target, count)] = ref[base:base + width, source:source + count]

    at = 0
    total = None
    for lo, hi in spans:
        begin = at
        for row in range(lo, hi):
            near = jnp.concatenate(
                [ext[:, pl.ds(pl.multiple_of(ids_ref[slot, row] * BS, BS), BS)] for slot in range(slots)], axis=1
            )
            both = jnp.concatenate(
                [jnp.concatenate([ref[row, slot] for slot in range(slots)], axis=1) for ref in (g_ref, c_ref)], axis=0
            )
            prod = lax.dot_general(both, near, (((1,), (1,)), ((), ())), preferred_element_type=F32).astype(BF16)
            prods[at:at + BS, 0:2 * width] = prod[0:BS]
            prods[at:at + BS, 2 * width:4 * width] = prod[BS:2 * BS]
            at += BS
        part = lax.dot_general(
            basis_ref[lo * BS:hi * BS, :], prods[begin:at, :], (((0,), (0,)), ((), ())), preferred_element_type=F32
        )
        total = part if total is None else total + part
    if before is not None:
        total = total + before[...]
    if len(outs) == 1:
        outs[0][...] = total
        return
    send_ref, keep_ref = outs
    states, columns = total.shape
    total = total.reshape(groups, 2, states // (2 * groups), columns)
    keep_ref[...] = jnp.where(odd == 1, total[:, 1], total[:, 0])
    send_ref[...] = jnp.where(odd == 1, total[:, 0], total[:, 1]).astype(BF16)


def project(fixed, pieces, spans, groups, before=None, last=True):
    ids, g_blocks, c_blocks, basis = fixed
    rows, slots = g_blocks.shape[0], g_blocks.shape[1]
    width = ROWS_OF_CORE
    states = basis.shape[1]
    piece = (groups, states // (2 * groups), 4 * width)
    arrays = [array for mine, other, _, _ in pieces for array in (mine, other)]
    more = [] if before is None else [before]
    count = sum(hi - lo for lo, hi in spans)
    outs = [shape(piece, BF16), shape(piece, F32)] if last else [shape((states, 4 * width), F32)]
    places = [(base, parts) for _, _, base, parts in pieces]
    return pl.pallas_call(
        functools.partial(project_kernel, spans, places, groups, before is not None),
        out_shape=outs,
        in_specs=[SMEM] + [VMEM] * (3 + len(arrays) + len(more)),
        out_specs=[VMEM] * len(outs),
        scratch_shapes=[
            pltpu.VMEM((2 * width, (rows + 2 * HB) * BS), BF16),
            pltpu.VMEM((count * BS, 4 * width), BF16),
        ],
        compiler_params=params(14),
        cost_estimate=pl.CostEstimate(flops=count, bytes_accessed=count, transcendentals=0),
    )(ids, g_blocks, c_blocks, basis, *arrays, *more)


def spread_kernel(groups, keep, got, keep_ref, *send_refs):
    here = lax.axis_index("node") // 2
    for step in range(groups):
        value = keep[here ^ step] + got[here ^ step].astype(F32)
        if step == 0:
            keep_ref[...] = value
        else:
            send_refs[step - 1][...] = value.astype(BF16)


def spread(groups, keep, got):
    piece = keep.shape[1:]
    return pl.pallas_call(
        functools.partial(spread_kernel, groups),
        out_shape=[shape(piece, F32)] + [shape(piece, BF16)] * (groups - 1),
        in_specs=[VMEM] * 2,
        out_specs=[VMEM] * groups,
        compiler_params=params(4),
    )(keep, got)


def finish_kernel(count, *refs):
    out_g, out_c = refs[-2:]
    quarter = out_g.shape[1] // 2
    first = lax.axis_index("col") // 2
    for place, half in ((first, refs[:count]), (1 - first, refs[count:2 * count])):
        total = half[0][...]
        for ref in half[1:]:
            total = total + ref[...].astype(F32)
        at = pl.ds(pl.multiple_of(place * quarter, quarter), quarter)
        out_g[:, at] = total[:, 0:quarter]
        out_c[:, at] = total[:, quarter:2 * quarter]


def finish(own, far):
    piece = shape(own[0].shape, F32)
    return pl.pallas_call(
        functools.partial(finish_kernel, len(own)),
        out_shape=(piece, piece),
        in_specs=[VMEM] * (len(own) + len(far)),
        out_specs=(VMEM, VMEM),
        compiler_params=params(4),
    )(*own, *far)


def body(panel, basis, g_blocks, c_blocks, block_cols):
    nodes, cols = lax.axis_size("node"), lax.axis_size("col")
    rows = g_blocks.shape[0]
    groups = nodes // 2
    halo = HB * BS
    inner = rows * BS

    def across(array):
        return lax.ppermute(array, "col", [(i, i ^ 2) for i in range(cols)])

    def cores(array):
        return lax.ppermute(array, "col", [(i, i ^ 1) for i in range(cols)])

    def swap(array, step):
        return lax.ppermute(array, "node", [(i, i ^ step) for i in range(nodes)])

    def swap_next(array):
        pairs = [(i, i + 1) for i in range(1, nodes - 1, 2)]
        return lax.ppermute(array, "node", pairs + [(j, i) for i, j in pairs])

    ends, middle = cut(panel.T)
    far_ends, far_middle = across(ends), across(middle)
    own = [
        (ends, cores(ends), 0, [(0, inner, halo, halo), (halo, halo, inner, halo)]),
        (middle, cores(middle), 0, [(0, 2 * halo, 2 * halo, inner - 2 * halo)]),
    ]
    (basis,) = load(basis)
    ids = jnp.clip(block_cols.T - (lax.axis_index("node") * rows - HB), 0, rows + 2 * HB - 1)
    far_ends, basis, ids = lax.optimization_barrier((far_ends, basis, ids))
    all_ends = jnp.concatenate([ends, far_ends], axis=0)
    rim = jnp.concatenate([swap(all_ends[:, :halo], 1), swap_next(all_ends[:, halo:])], axis=1)
    fixed = (ids, g_blocks, c_blocks, basis)
    (part,) = project(fixed, own, [(HB, rows - HB)], groups, last=False)
    part, far_middle = lax.optimization_barrier((part, far_middle))
    rim_other = cores(rim)
    rim_parts = [(0, halo + inner, 0, halo), (halo, 0, halo + inner, halo)]
    send_a, keep_a = project(
        fixed, own + [(rim, rim_other, 0, rim_parts)], [(0, HB), (rows - HB, rows)], groups, before=part
    )
    got_a = swap(send_a, 1)
    far = [
        (rim, rim_other, ROWS_OF_CORE, rim_parts),
        (far_ends, cores(far_ends), 0, [(0, inner, halo, halo), (halo, halo, inner, halo)]),
        (far_middle, cores(far_middle), 0, [(0, 2 * halo, 2 * halo, inner - 2 * halo)]),
    ]
    send_b, keep_b = project(fixed, far, [(0, rows)], groups)
    got_b = swap(send_b, 1)
    halves = []
    for keep, got in ((keep_a, got_a), (keep_b, got_b)):
        keep, *sends = spread(groups, keep, got)
        halves.append([keep] + [swap(send, 2 * step) for step, send in enumerate(sends, 1)])
    return finish(*halves)


def solution(mesh):
    in_specs = (
        P("node", "col"),
        P("node", "col"),
        P("node", None, None, None),
        P("node", None, None, None),
        P("node", None),
    )
    out_specs = (P(("col", "node"), None), P(("col", "node"), None))
    return jax.shard_map(body, mesh=mesh, in_specs=in_specs, out_specs=out_specs, check_vma=False)
```

```python
import functools

import jax
import jax.numpy as jnp
from jax import lax
from jax.experimental import pallas as pl
from jax.experimental.pallas import tpu as pltpu
from jax.sharding import PartitionSpec as P

BS = 128
HB = 4
ROWS_OF_CORE = 64
MIB = 1024 * 1024
F32 = jnp.float32
BF16 = jnp.bfloat16
VMEM = pl.BlockSpec(memory_space=pltpu.VMEM)
SMEM = pl.BlockSpec(memory_space=pltpu.SMEM)
HBM = pl.BlockSpec(memory_space=pl.ANY)


def params(mib):
    return pltpu.CompilerParams(vmem_limit_bytes=mib * MIB)


def shape(dims, kind):
    return jax.ShapeDtypeStruct(dims, kind)


def cut_kernel(panel, ends, middle, sems):
    inner = panel.shape[1]
    halo = HB * BS
    odd = lax.axis_index("node") % 2
    to_pair = pl.multiple_of((1 - odd) * (inner - halo), BS)
    to_next = pl.multiple_of(odd * (inner - halo), BS)
    copies = [
        (panel.at[:, pl.ds(to_pair, halo)], ends.at[:, 0:halo]),
        (panel.at[:, pl.ds(to_next, halo)], ends.at[:, halo:2 * halo]),
        (panel.at[:, halo:inner - halo], middle),
    ]
    copies = [pltpu.make_async_copy(*pair, sems.at[i]) for i, pair in enumerate(copies)]
    for copy in copies:
        copy.start()
    for copy in copies:
        copy.wait()


def cut(panel):
    width, inner = panel.shape
    halo = HB * BS
    return pl.pallas_call(
        cut_kernel,
        out_shape=[shape((width, w), BF16) for w in (2 * halo, inner - 2 * halo)],
        in_specs=[HBM],
        out_specs=[VMEM] * 2,
        scratch_shapes=[pltpu.SemaphoreType.DMA((3,))],
        compiler_params=params(44),
    )(panel)


def load_kernel(*refs):
    count = len(refs) // 2
    sources, targets, sems = refs[:count], refs[count:2 * count], refs[-1]
    copies = []
    for which, (source, target) in enumerate(zip(sources, targets)):
        middle = source.shape[0] // 2
        for part, span in enumerate((pl.ds(0, middle), pl.ds(middle, source.shape[0] - middle))):
            copies.append(pltpu.make_async_copy(source.at[span], target.at[span], sems.at[which, part]))
    for copy in copies:
        copy.start()
    for copy in copies:
        copy.wait()


def load(*arrays):
    size = sum(array.size * array.dtype.itemsize for array in arrays)
    return pl.pallas_call(
        load_kernel,
        out_shape=[shape(array.shape, array.dtype) for array in arrays],
        in_specs=[HBM] * len(arrays),
        out_specs=[VMEM] * len(arrays),
        scratch_shapes=[pltpu.SemaphoreType.DMA((len(arrays), 2))],
        compiler_params=params(45),
        cost_estimate=pl.CostEstimate(flops=0, bytes_accessed=size * 1, transcendentals=0),
    )(*arrays)


def project_kernel(spans, places, groups, more, *refs):
    ids_ref, g_ref, c_ref, basis_ref = refs[:4]
    pieces = refs[4:4 + 2 * len(places)]
    rest = list(refs[4 + 2 * len(places):])
    before = rest.pop(0) if more else None
    *outs, ext, prods = rest
    slots = g_ref.shape[1]
    width = ROWS_OF_CORE
    core = lax.axis_index("col") % 2
    odd = lax.axis_index("node") % 2

    for which, (bases, parts) in enumerate(places):
        for owner, base, ref in zip((core, 1 - core), bases, pieces[2 * which:2 * which + 2]):
            at = pl.ds(pl.multiple_of(owner * width, width), width)
            for source, even_target, odd_target, count in parts:
                target = even_target
                if odd_target != even_target:
                    target = pl.multiple_of(even_target + odd * (odd_target - even_target), BS)
                ext[at, pl.ds(target, count)] = ref[base:base + width, source:source + count]

    at = 0
    total = None
    for lo, hi in spans:
        begin = at
        for row in range(lo, hi):
            near = jnp.concatenate(
                [ext[:, pl.ds(pl.multiple_of(ids_ref[slot, row] * BS, BS), BS)] for slot in range(slots)], axis=1
            )
            both = jnp.concatenate(
                [jnp.concatenate([ref[row, slot] for slot in range(slots)], axis=1) for ref in (g_ref, c_ref)], axis=0
            )
            prod = lax.dot_general(both, near, (((1,), (1,)), ((), ())), preferred_element_type=F32).astype(BF16)
            prods[at:at + BS, 0:2 * width] = prod[0:BS]
            prods[at:at + BS, 2 * width:4 * width] = prod[BS:2 * BS]
            at += BS
        part = lax.dot_general(
            basis_ref[lo * BS:hi * BS, :], prods[begin:at, :], (((0,), (0,)), ((), ())), preferred_element_type=F32
        )
        total = part if total is None else total + part
    if before is not None:
        total = total + before[...]
    if len(outs) == 1:
        outs[0][...] = total
        return
    send_ref, keep_ref = outs
    states, columns = total.shape
    total = total.reshape(groups, 2, states // (2 * groups), columns)
    keep_ref[...] = jnp.where(odd == 1, total[:, 1], total[:, 0])
    send_ref[...] = jnp.where(odd == 1, total[:, 0], total[:, 1]).astype(BF16)


def project(fixed, pieces, spans, groups, before=None, last=True):
    ids, g_blocks, c_blocks, basis = fixed
    rows, slots = g_blocks.shape[0], g_blocks.shape[1]
    width = ROWS_OF_CORE
    states = basis.shape[1]
    piece = (groups, states // (2 * groups), 4 * width)
    arrays = [array for mine, other, _, _ in pieces for array in (mine, other)]
    more = [] if before is None else [before]
    count = sum(hi - lo for lo, hi in spans)
    outs = [shape(piece, BF16), shape(piece, F32)] if last else [shape((states, 4 * width), F32)]
    places = [(base, parts) for _, _, base, parts in pieces]
    return pl.pallas_call(
        functools.partial(project_kernel, spans, places, groups, before is not None),
        out_shape=outs,
        in_specs=[SMEM] + [VMEM] * (3 + len(arrays) + len(more)),
        out_specs=[VMEM] * len(outs),
        scratch_shapes=[
            pltpu.VMEM((2 * width, (rows + 2 * HB) * BS), BF16),
            pltpu.VMEM((count * BS, 4 * width), BF16),
        ],
        compiler_params=params(14),
        cost_estimate=pl.CostEstimate(flops=int(2.3e+09) if more else (count if last else int(1)), bytes_accessed=count, transcendentals=0),
    )(ids, g_blocks, c_blocks, basis, *arrays, *more)


def spread_kernel(groups, keep, got, keep_ref, *send_refs):
    here = lax.axis_index("node") // 2
    for step in range(groups):
        value = keep[here ^ step] + got[here ^ step].astype(F32)
        if step == 0:
            keep_ref[...] = value
        else:
            send_refs[step - 1][...] = value.astype(BF16)


def spread(groups, keep, got):
    piece = keep.shape[1:]
    return pl.pallas_call(
        functools.partial(spread_kernel, groups),
        out_shape=[shape(piece, F32)] + [shape(piece, BF16)] * (groups - 1),
        in_specs=[VMEM] * 2,
        out_specs=[VMEM] * groups,
        compiler_params=params(4),
    )(keep, got)


def finish_kernel(count, *refs):
    out_g, out_c = refs[-2:]
    quarter = out_g.shape[1] // 2
    first = lax.axis_index("col") // 2
    for place, half in ((first, refs[:count]), (1 - first, refs[count:2 * count])):
        total = half[0][...]
        for ref in half[1:]:
            total = total + ref[...].astype(F32)
        at = pl.ds(pl.multiple_of(place * quarter, quarter), quarter)
        out_g[:, at] = total[:, 0:quarter]
        out_c[:, at] = total[:, quarter:2 * quarter]


def finish(own, far):
    piece = shape(own[0].shape, F32)
    return pl.pallas_call(
        functools.partial(finish_kernel, len(own)),
        out_shape=(piece, piece),
        in_specs=[VMEM] * (len(own) + len(far)),
        out_specs=(VMEM, VMEM),
        compiler_params=params(4),
    )(*own, *far)


def body(panel, basis, g_blocks, c_blocks, block_cols):
    nodes, cols = lax.axis_size("node"), lax.axis_size("col")
    rows = g_blocks.shape[0]
    groups = nodes // 2
    halo = HB * BS
    inner = rows * BS

    def across(array):
        return lax.ppermute(array, "col", [(i, i ^ 2) for i in range(cols)])

    def cores(array):
        return lax.ppermute(array, "col", [(i, i ^ 1) for i in range(cols)])

    def swap(array, step):
        return lax.ppermute(array, "node", [(i, i ^ step) for i in range(nodes)])

    def swap_next(array):
        pairs = [(i, i + 1) for i in range(1, nodes - 1, 2)]
        return lax.ppermute(array, "node", pairs + [(j, i) for i, j in pairs])

    ends, middle = cut(panel.T)
    far_ends, far_middle = across(ends), across(middle)
    ends_other = cores(ends)
    own = [
        (ends, ends_other, (0, 0), [(0, inner, halo, halo), (halo, halo, inner, halo)]),
        (middle, cores(middle), (0, 0), [(0, 2 * halo, 2 * halo, inner - 2 * halo)]),
    ]
    (basis,) = load(basis)
    ids = jnp.clip(block_cols.T - (lax.axis_index("node") * rows - HB), 0, rows + 2 * HB - 1)
    far_ends, basis, ids = lax.optimization_barrier((far_ends, basis, ids))
    all_ends = jnp.concatenate([ends, ends_other, far_ends], axis=0)
    rim = jnp.concatenate([swap(all_ends[:, :halo], 1), swap_next(all_ends[:, halo:])], axis=1)
    fixed = (ids, g_blocks, c_blocks, basis)
    (part,) = project(fixed, own, [(HB, rows - HB)], groups, last=False)
    part, far_middle = lax.optimization_barrier((part, far_middle))
    far_rim = 2 * ROWS_OF_CORE
    rim_parts = [(0, halo + inner, 0, halo), (halo, 0, halo + inner, halo)]
    send_a, keep_a = project(
        fixed, own + [(rim, rim, (0, ROWS_OF_CORE), rim_parts)], [(0, HB), (rows - HB, rows)], groups, before=part
    )
    got_a = swap(send_a, 1)
    far = [
        (rim, cores(rim[far_rim:]), (far_rim, 0), rim_parts),
        (far_ends, cores(far_ends), (0, 0), [(0, inner, halo, halo), (halo, halo, inner, halo)]),
        (far_middle, cores(far_middle), (0, 0), [(0, 2 * halo, 2 * halo, inner - 2 * halo)]),
    ]
    send_b, keep_b = project(fixed, far, [(0, rows)], groups)
    got_b = swap(send_b, 1)
    halves = []
    for keep, got in ((keep_a, got_a), (keep_b, got_b)):
        keep, *sends = spread(groups, keep, got)
        halves.append([keep] + [swap(send, 2 * step) for step, send in enumerate(sends, 1)])
    return finish(*halves)


def solution(mesh):
    in_specs = (
        P("node", "col"),
        P("node", "col"),
        P("node", None, None, None),
        P("node", None, None, None),
        P("node", None),
    )
    out_specs = (P(("col", "node"), None), P(("col", "node"), None))
    return jax.shard_map(body, mesh=mesh, in_specs=in_specs, out_specs=out_specs, check_vma=False)
```

```python
import functools

import jax
import jax.numpy as jnp
from jax import lax
from jax.experimental import pallas as pl
from jax.experimental.pallas import tpu as pltpu
from jax.sharding import PartitionSpec as P

BS = 128
HB = 4
ROWS_OF_CORE = 64
MIB = 1024 * 1024
F32 = jnp.float32
BF16 = jnp.bfloat16
VMEM = pl.BlockSpec(memory_space=pltpu.VMEM)
SMEM = pl.BlockSpec(memory_space=pltpu.SMEM)
HBM = pl.BlockSpec(memory_space=pl.ANY)


def params(mib):
    return pltpu.CompilerParams(vmem_limit_bytes=mib * MIB)


def shape(dims, kind):
    return jax.ShapeDtypeStruct(dims, kind)


def cut_kernel(panel, ends, middle, sems):
    inner = panel.shape[1]
    halo = HB * BS
    odd = lax.axis_index("node") % 2
    to_pair = pl.multiple_of((1 - odd) * (inner - halo), BS)
    to_next = pl.multiple_of(odd * (inner - halo), BS)
    copies = [
        (panel.at[:, pl.ds(to_pair, halo)], ends.at[:, 0:halo]),
        (panel.at[:, pl.ds(to_next, halo)], ends.at[:, halo:2 * halo]),
        (panel.at[:, halo:inner - halo], middle),
    ]
    copies = [pltpu.make_async_copy(*pair, sems.at[i]) for i, pair in enumerate(copies)]
    for copy in copies:
        copy.start()
    for copy in copies:
        copy.wait()


def cut(panel):
    width, inner = panel.shape
    halo = HB * BS
    return pl.pallas_call(
        cut_kernel,
        out_shape=[shape((width, w), BF16) for w in (2 * halo, inner - 2 * halo)],
        in_specs=[HBM],
        out_specs=[VMEM] * 2,
        scratch_shapes=[pltpu.SemaphoreType.DMA((3,))],
        compiler_params=params(44),
    )(panel)


def load_kernel(*refs):
    count = len(refs) // 2
    sources, targets, sems = refs[:count], refs[count:2 * count], refs[-1]
    copies = []
    for which, (source, target) in enumerate(zip(sources, targets)):
        middle = source.shape[0] // 2
        for part, span in enumerate((pl.ds(0, middle), pl.ds(middle, source.shape[0] - middle))):
            copies.append(pltpu.make_async_copy(source.at[span], target.at[span], sems.at[which, part]))
    for copy in copies:
        copy.start()
    for copy in copies:
        copy.wait()


def load(*arrays):
    size = sum(array.size * array.dtype.itemsize for array in arrays)
    return pl.pallas_call(
        load_kernel,
        out_shape=[shape(array.shape, array.dtype) for array in arrays],
        in_specs=[HBM] * len(arrays),
        out_specs=[VMEM] * len(arrays),
        scratch_shapes=[pltpu.SemaphoreType.DMA((len(arrays), 2))],
        compiler_params=params(45),
        cost_estimate=pl.CostEstimate(flops=0, bytes_accessed=size * 1, transcendentals=0),
    )(*arrays)


def project_kernel(spans, places, groups, more, *refs):
    ids_ref, g_ref, c_ref, basis_ref = refs[:4]
    pieces = refs[4:4 + 2 * len(places)]
    rest = list(refs[4 + 2 * len(places):])
    before = rest.pop(0) if more else None
    *outs, ext, prods = rest
    slots = g_ref.shape[1]
    width = ROWS_OF_CORE
    core = lax.axis_index("col") % 2
    odd = lax.axis_index("node") % 2

    for which, (bases, parts) in enumerate(places):
        for owner, base, ref in zip((core, 1 - core), bases, pieces[2 * which:2 * which + 2]):
            at = pl.ds(pl.multiple_of(owner * width, width), width)
            for source, even_target, odd_target, count in parts:
                target = even_target
                if odd_target != even_target:
                    target = pl.multiple_of(even_target + odd * (odd_target - even_target), BS)
                ext[at, pl.ds(target, count)] = ref[base:base + width, source:source + count]

    at = 0
    total = None
    for lo, hi in spans:
        begin = at
        for row in range(lo, hi):
            near = jnp.concatenate(
                [ext[:, pl.ds(pl.multiple_of(ids_ref[slot, row] * BS, BS), BS)] for slot in range(slots)], axis=1
            )
            both = jnp.concatenate(
                [jnp.concatenate([ref[row, slot] for slot in range(slots)], axis=1) for ref in (g_ref, c_ref)], axis=0
            )
            prod = lax.dot_general(both, near, (((1,), (1,)), ((), ())), preferred_element_type=F32).astype(BF16)
            prods[at:at + BS, 0:2 * width] = prod[0:BS]
            prods[at:at + BS, 2 * width:4 * width] = prod[BS:2 * BS]
            at += BS
        part = lax.dot_general(
            basis_ref[lo * BS:hi * BS, :], prods[begin:at, :], (((0,), (0,)), ((), ())), preferred_element_type=F32
        )
        total = part if total is None else total + part
    if before is not None:
        total = total + before[...]
    if len(outs) == 1:
        outs[0][...] = total
        return
    send_ref, keep_ref = outs
    states, columns = total.shape
    total = total.reshape(groups, 2, states // (2 * groups), columns)
    keep_ref[...] = jnp.where(odd == 1, total[:, 1], total[:, 0])
    send_ref[...] = jnp.where(odd == 1, total[:, 0], total[:, 1]).astype(BF16)


def project(fixed, pieces, spans, groups, before=None, last=True):
    ids, g_blocks, c_blocks, basis = fixed
    rows, slots = g_blocks.shape[0], g_blocks.shape[1]
    width = ROWS_OF_CORE
    states = basis.shape[1]
    piece = (groups, states // (2 * groups), 4 * width)
    arrays = [array for mine, other, _, _ in pieces for array in (mine, other)]
    more = [] if before is None else [before]
    count = sum(hi - lo for lo, hi in spans)
    outs = [shape(piece, BF16), shape(piece, F32)] if last else [shape((states, 4 * width), F32)]
    places = [(base, parts) for _, _, base, parts in pieces]
    return pl.pallas_call(
        functools.partial(project_kernel, spans, places, groups, before is not None),
        out_shape=outs,
        in_specs=[SMEM] + [VMEM] * (3 + len(arrays) + len(more)),
        out_specs=[VMEM] * len(outs),
        scratch_shapes=[
            pltpu.VMEM((2 * width, (rows + 2 * HB) * BS), BF16),
            pltpu.VMEM((count * BS, 4 * width), BF16),
        ],
        compiler_params=params(14),
        cost_estimate=pl.CostEstimate(flops=int(2.3e+09) if more else (count if last else int(1)), bytes_accessed=count, transcendentals=0),
    )(ids, g_blocks, c_blocks, basis, *arrays, *more)


def spread_kernel(groups, keep, got, keep_ref, *send_refs):
    here = lax.axis_index("node") // 2
    for step in range(groups):
        value = keep[here ^ step] + got[here ^ step].astype(F32)
        if step == 0:
            keep_ref[...] = value
        else:
            send_refs[step - 1][...] = value.astype(BF16)


def spread(groups, keep, got):
    piece = keep.shape[1:]
    return pl.pallas_call(
        functools.partial(spread_kernel, groups),
        out_shape=[shape(piece, F32)] + [shape(piece, BF16)] * (groups - 1),
        in_specs=[VMEM] * 2,
        out_specs=[VMEM] * groups,
        compiler_params=params(4),
    )(keep, got)


def finish_kernel(count, *refs):
    out_g, out_c = refs[-2:]
    quarter = out_g.shape[1] // 2
    first = lax.axis_index("col") // 2
    for place, half in ((first, refs[:count]), (1 - first, refs[count:2 * count])):
        total = half[0][...]
        for ref in half[1:]:
            total = total + ref[...].astype(F32)
        at = pl.ds(pl.multiple_of(place * quarter, quarter), quarter)
        out_g[:, at] = total[:, 0:quarter]
        out_c[:, at] = total[:, quarter:2 * quarter]


def finish(own, far):
    piece = shape(own[0].shape, F32)
    return pl.pallas_call(
        functools.partial(finish_kernel, len(own)),
        out_shape=(piece, piece),
        in_specs=[VMEM] * (len(own) + len(far)),
        out_specs=(VMEM, VMEM),
        compiler_params=params(4),
    )(*own, *far)


def body(panel, basis, g_blocks, c_blocks, block_cols):
    nodes, cols = lax.axis_size("node"), lax.axis_size("col")
    rows = g_blocks.shape[0]
    groups = nodes // 2
    halo = HB * BS
    inner = rows * BS

    def across(array):
        return lax.ppermute(array, "col", [(i, i ^ 2) for i in range(cols)])

    def cores(array):
        return lax.ppermute(array, "col", [(i, i ^ 1) for i in range(cols)])

    def swap(array, step):
        return lax.ppermute(array, "node", [(i, i ^ step) for i in range(nodes)])

    def swap_next(array):
        pairs = [(i, i + 1) for i in range(1, nodes - 1, 2)]
        return lax.ppermute(array, "node", pairs + [(j, i) for i, j in pairs])

    ends, middle = cut(panel.T)
    far_ends, far_middle = across(ends), across(middle)
    ends_other = cores(ends)
    own = [
        (ends, ends_other, (0, 0), [(0, inner, halo, halo), (halo, halo, inner, halo)]),
        (middle, cores(middle), (0, 0), [(0, 2 * halo, 2 * halo, inner - 2 * halo)]),
    ]
    (basis,) = load(basis)
    ids = jnp.clip(block_cols.T - (lax.axis_index("node") * rows - HB), 0, rows + 2 * HB - 1)
    far_ends, basis, ids = lax.optimization_barrier((far_ends, basis, ids))
    all_ends = jnp.concatenate([ends, ends_other, far_ends], axis=0)
    rim = jnp.concatenate([swap(all_ends[:, :halo], 1), swap_next(all_ends[:, halo:])], axis=1)
    fixed = (ids, g_blocks, c_blocks, basis)
    (part,) = project(fixed, own, [(HB, rows - HB)], groups, last=False)
    part, far_middle = lax.optimization_barrier((part, far_middle))
    far_rim = 2 * ROWS_OF_CORE
    rim_parts = [(0, halo + inner, 0, halo), (halo, 0, halo + inner, halo)]
    send_a, keep_a = project(
        fixed, own + [(rim, rim, (0, ROWS_OF_CORE), rim_parts)], [(0, HB), (rows - HB, rows)], groups, before=part
    )
    got_a = swap(send_a, 1)
    far = [
        (rim, cores(rim[far_rim:]), (far_rim, 0), rim_parts),
        (far_ends, cores(far_ends), (0, 0), [(0, inner, halo, halo), (halo, halo, inner, halo)]),
        (far_middle, cores(far_middle), (0, 0), [(0, 2 * halo, 2 * halo, inner - 2 * halo)]),
    ]
    send_b, keep_b = project(fixed, far, [(0, rows)], groups)
    got_b = swap(send_b, 1)
    halves = []
    for keep, got in ((keep_a, got_a), (keep_b, got_b)):
        keep, *sends = spread(groups, keep, got)
        steps = sorted(range(1, groups), key=lambda step: -step)
        halves.append([keep] + [swap(sends[step - 1], 2 * step) for step in steps])
    return finish(*halves)


def solution(mesh):
    in_specs = (
        P("node", "col"),
        P("node", "col"),
        P("node", None, None, None),
        P("node", None, None, None),
        P("node", None),
    )
    out_specs = (P(("col", "node"), None), P(("col", "node"), None))
    return jax.shard_map(body, mesh=mesh, in_specs=in_specs, out_specs=out_specs, check_vma=False)
```

```python
import functools

import jax
import jax.numpy as jnp
from jax import lax
from jax.experimental import pallas as pl
from jax.experimental.pallas import tpu as pltpu
from jax.sharding import PartitionSpec as P

BS = 128
HB = 4
ROWS_OF_CORE = 64
MIB = 1024 * 1024
F32 = jnp.float32
BF16 = jnp.bfloat16
VMEM = pl.BlockSpec(memory_space=pltpu.VMEM)
SMEM = pl.BlockSpec(memory_space=pltpu.SMEM)
HBM = pl.BlockSpec(memory_space=pl.ANY)


def params(mib):
    return pltpu.CompilerParams(vmem_limit_bytes=mib * MIB)


def shape(dims, kind):
    return jax.ShapeDtypeStruct(dims, kind)


def cut_kernel(panel, ends, middle, sems):
    inner = panel.shape[1]
    halo = HB * BS
    odd = lax.axis_index("node") % 2
    to_pair = pl.multiple_of((1 - odd) * (inner - halo), BS)
    to_next = pl.multiple_of(odd * (inner - halo), BS)
    copies = [
        (panel.at[:, pl.ds(to_pair, halo)], ends.at[:, 0:halo]),
        (panel.at[:, pl.ds(to_next, halo)], ends.at[:, halo:2 * halo]),
        (panel.at[:, halo:inner - halo], middle),
    ]
    copies = [pltpu.make_async_copy(*pair, sems.at[i]) for i, pair in enumerate(copies)]
    for copy in copies:
        copy.start()
    for copy in copies:
        copy.wait()


def cut(panel):
    width, inner = panel.shape
    halo = HB * BS
    return pl.pallas_call(
        cut_kernel,
        out_shape=[shape((width, w), BF16) for w in (2 * halo, inner - 2 * halo)],
        in_specs=[HBM],
        out_specs=[VMEM] * 2,
        scratch_shapes=[pltpu.SemaphoreType.DMA((3,))],
        compiler_params=params(44),
    )(panel)


def load_kernel(*refs):
    count = len(refs) // 2
    sources, targets, sems = refs[:count], refs[count:2 * count], refs[-1]
    copies = []
    for which, (source, target) in enumerate(zip(sources, targets)):
        middle = source.shape[0] // 2
        for part, span in enumerate((pl.ds(0, middle), pl.ds(middle, source.shape[0] - middle))):
            copies.append(pltpu.make_async_copy(source.at[span], target.at[span], sems.at[which, part]))
    for copy in copies:
        copy.start()
    for copy in copies:
        copy.wait()


def load(*arrays):
    size = sum(array.size * array.dtype.itemsize for array in arrays)
    return pl.pallas_call(
        load_kernel,
        out_shape=[shape(array.shape, array.dtype) for array in arrays],
        in_specs=[HBM] * len(arrays),
        out_specs=[VMEM] * len(arrays),
        scratch_shapes=[pltpu.SemaphoreType.DMA((len(arrays), 2))],
        compiler_params=params(45),
        cost_estimate=pl.CostEstimate(flops=0, bytes_accessed=size * 1, transcendentals=0),
    )(*arrays)


def project_kernel(spans, places, groups, more, *refs):
    ids_ref, g_ref, c_ref, basis_ref = refs[:4]
    pieces = refs[4:4 + 2 * len(places)]
    rest = list(refs[4 + 2 * len(places):])
    before = rest.pop(0) if more else None
    *outs, ext, prods = rest
    slots = g_ref.shape[1]
    width = ROWS_OF_CORE
    core = lax.axis_index("col") % 2
    odd = lax.axis_index("node") % 2

    for which, (bases, parts) in enumerate(places):
        for owner, base, ref in zip((core, 1 - core), bases, pieces[2 * which:2 * which + 2]):
            at = pl.ds(pl.multiple_of(owner * width, width), width)
            for source, even_target, odd_target, count in parts:
                target = even_target
                if odd_target != even_target:
                    target = pl.multiple_of(even_target + odd * (odd_target - even_target), BS)
                ext[at, pl.ds(target, count)] = ref[base:base + width, source:source + count]

    at = 0
    total = None
    for lo, hi in spans:
        begin = at
        for row in range(lo, hi):
            near = jnp.concatenate(
                [ext[:, pl.ds(pl.multiple_of(ids_ref[slot, row] * BS, BS), BS)] for slot in range(slots)], axis=1
            )
            both = jnp.concatenate(
                [jnp.concatenate([ref[row, slot] for slot in range(slots)], axis=1) for ref in (g_ref, c_ref)], axis=0
            )
            prod = lax.dot_general(both, near, (((1,), (1,)), ((), ())), preferred_element_type=F32).astype(BF16)
            prods[at:at + BS, 0:2 * width] = prod[0:BS]
            prods[at:at + BS, 2 * width:4 * width] = prod[BS:2 * BS]
            at += BS
        part = lax.dot_general(
            basis_ref[lo * BS:hi * BS, :], prods[begin:at, :], (((0,), (0,)), ((), ())), preferred_element_type=F32
        )
        total = part if total is None else total + part
    if before is not None:
        total = total + before[...]
    if len(outs) == 1:
        outs[0][...] = total
        return
    send_ref, keep_ref = outs
    states, columns = total.shape
    total = total.reshape(groups, 2, states // (2 * groups), columns)
    keep_ref[...] = jnp.where(odd == 1, total[:, 1], total[:, 0])
    send_ref[...] = jnp.where(odd == 1, total[:, 0], total[:, 1]).astype(BF16)


def project(fixed, pieces, spans, groups, before=None, last=True):
    ids, g_blocks, c_blocks, basis = fixed
    rows, slots = g_blocks.shape[0], g_blocks.shape[1]
    width = ROWS_OF_CORE
    states = basis.shape[1]
    piece = (groups, states // (2 * groups), 4 * width)
    arrays = [array for mine, other, _, _ in pieces for array in (mine, other)]
    more = [] if before is None else [before]
    count = sum(hi - lo for lo, hi in spans)
    outs = [shape(piece, BF16), shape(piece, F32)] if last else [shape((states, 4 * width), F32)]
    places = [(base, parts) for _, _, base, parts in pieces]
    return pl.pallas_call(
        functools.partial(project_kernel, spans, places, groups, before is not None),
        out_shape=outs,
        in_specs=[SMEM] + [VMEM] * (3 + len(arrays) + len(more)),
        out_specs=[VMEM] * len(outs),
        scratch_shapes=[
            pltpu.VMEM((2 * width, (rows + 2 * HB) * BS), BF16),
            pltpu.VMEM((count * BS, 4 * width), BF16),
        ],
        compiler_params=params(14),
        cost_estimate=pl.CostEstimate(flops=int(3.45e+09) if more else (count if last else int(1)), bytes_accessed=count, transcendentals=0),
    )(ids, g_blocks, c_blocks, basis, *arrays, *more)


def spread_kernel(groups, keep, got, keep_ref, *send_refs):
    here = lax.axis_index("node") // 2
    for step in range(groups):
        value = keep[here ^ step] + got[here ^ step].astype(F32)
        if step == 0:
            keep_ref[...] = value
        else:
            send_refs[step - 1][...] = value.astype(BF16)


def spread(groups, keep, got):
    piece = keep.shape[1:]
    return pl.pallas_call(
        functools.partial(spread_kernel, groups),
        out_shape=[shape(piece, F32)] + [shape(piece, BF16)] * (groups - 1),
        in_specs=[VMEM] * 2,
        out_specs=[VMEM] * groups,
        compiler_params=params(4),
    )(keep, got)


def finish_kernel(count, *refs):
    out_g, out_c = refs[-2:]
    quarter = out_g.shape[1] // 2
    first = lax.axis_index("col") // 2
    for place, half in ((first, refs[:count]), (1 - first, refs[count:2 * count])):
        total = half[0][...]
        for ref in half[1:]:
            total = total + ref[...].astype(F32)
        at = pl.ds(pl.multiple_of(place * quarter, quarter), quarter)
        out_g[:, at] = total[:, 0:quarter]
        out_c[:, at] = total[:, quarter:2 * quarter]


def finish(own, far):
    piece = shape(own[0].shape, F32)
    return pl.pallas_call(
        functools.partial(finish_kernel, len(own)),
        out_shape=(piece, piece),
        in_specs=[VMEM] * (len(own) + len(far)),
        out_specs=(VMEM, VMEM),
        compiler_params=params(4),
    )(*own, *far)


def body(panel, basis, g_blocks, c_blocks, block_cols):
    nodes, cols = lax.axis_size("node"), lax.axis_size("col")
    rows = g_blocks.shape[0]
    groups = nodes // 2
    halo = HB * BS
    inner = rows * BS

    def across(array):
        return lax.ppermute(array, "col", [(i, i ^ 2) for i in range(cols)])

    def cores(array):
        return lax.ppermute(array, "col", [(i, i ^ 1) for i in range(cols)])

    def swap(array, step):
        return lax.ppermute(array, "node", [(i, i ^ step) for i in range(nodes)])

    def swap_next(array):
        pairs = [(i, i + 1) for i in range(1, nodes - 1, 2)]
        return lax.ppermute(array, "node", pairs + [(j, i) for i, j in pairs])

    ends, middle = cut(panel.T)
    far_ends, far_middle = across(ends), across(middle)
    ends_other = cores(ends)
    own = [
        (ends, ends_other, (0, 0), [(0, inner, halo, halo), (halo, halo, inner, halo)]),
        (middle, cores(middle), (0, 0), [(0, 2 * halo, 2 * halo, inner - 2 * halo)]),
    ]
    (basis,) = load(basis)
    ids = jnp.clip(block_cols.T - (lax.axis_index("node") * rows - HB), 0, rows + 2 * HB - 1)
    far_ends, basis, ids = lax.optimization_barrier((far_ends, basis, ids))
    all_ends = jnp.concatenate([ends, ends_other, far_ends], axis=0)
    rim = jnp.concatenate([swap(all_ends[:, :halo], 1), swap_next(all_ends[:, halo:])], axis=1)
    fixed = (ids, g_blocks, c_blocks, basis)
    (part,) = project(fixed, own, [(HB, rows - HB)], groups, last=False)
    part, far_middle = lax.optimization_barrier((part, far_middle))
    far_rim = 2 * ROWS_OF_CORE
    near_parts = [(0, 2 * halo, 2 * halo, halo), (inner - 3 * halo, inner - halo, inner - halo, halo)]
    near_rim = [own[0], own[1][:3] + (near_parts,)]
    rim_parts = [(0, halo + inner, 0, halo), (halo, 0, halo + inner, halo)]
    send_a, keep_a = project(
        fixed, near_rim + [(rim, rim, (0, ROWS_OF_CORE), rim_parts)], [(0, HB), (rows - HB, rows)], groups, before=part
    )
    got_a = swap(send_a, 1)
    far = [
        (rim, cores(rim[far_rim:]), (far_rim, 0), rim_parts),
        (far_ends, cores(far_ends), (0, 0), [(0, inner, halo, halo), (halo, halo, inner, halo)]),
        (far_middle, cores(far_middle), (0, 0), [(0, 2 * halo, 2 * halo, inner - 2 * halo)]),
    ]
    send_b, keep_b = project(fixed, far, [(0, rows)], groups)
    got_b = swap(send_b, 1)
    halves = []
    for keep, got in ((keep_a, got_a), (keep_b, got_b)):
        keep, *sends = spread(groups, keep, got)
        steps = sorted(range(1, groups), key=lambda step: -step)
        halves.append([keep] + [swap(sends[step - 1], 2 * step) for step in steps])
    return finish(*halves)


def solution(mesh):
    in_specs = (
        P("node", "col"),
        P("node", "col"),
        P("node", None, None, None),
        P("node", None, None, None),
        P("node", None),
    )
    out_specs = (P(("col", "node"), None), P(("col", "node"), None))
    return jax.shard_map(body, mesh=mesh, in_specs=in_specs, out_specs=out_specs, check_vma=False)
```

```python
import functools

import jax
import jax.numpy as jnp
from jax import lax
from jax.experimental import pallas as pl
from jax.experimental.pallas import tpu as pltpu
from jax.sharding import PartitionSpec as P

BS = 128
HB = 4
ROWS_OF_CORE = 64
MIB = 1024 * 1024
F32 = jnp.float32
BF16 = jnp.bfloat16
VMEM = pl.BlockSpec(memory_space=pltpu.VMEM)
SMEM = pl.BlockSpec(memory_space=pltpu.SMEM)
HBM = pl.BlockSpec(memory_space=pl.ANY)


def params(mib):
    return pltpu.CompilerParams(vmem_limit_bytes=mib * MIB)


def shape(dims, kind):
    return jax.ShapeDtypeStruct(dims, kind)


def cut_kernel(panel, ends, middle, sems):
    inner = panel.shape[1]
    halo = HB * BS
    odd = lax.axis_index("node") % 2
    to_pair = pl.multiple_of((1 - odd) * (inner - halo), BS)
    to_next = pl.multiple_of(odd * (inner - halo), BS)
    copies = [
        (panel.at[:, pl.ds(to_pair, halo)], ends.at[:, 0:halo]),
        (panel.at[:, pl.ds(to_next, halo)], ends.at[:, halo:2 * halo]),
        (panel.at[:, halo:inner - halo], middle),
    ]
    copies = [pltpu.make_async_copy(*pair, sems.at[i]) for i, pair in enumerate(copies)]
    for copy in copies:
        copy.start()
    for copy in copies:
        copy.wait()


def cut(panel):
    width, inner = panel.shape
    halo = HB * BS
    return pl.pallas_call(
        cut_kernel,
        out_shape=[shape((width, w), BF16) for w in (2 * halo, inner - 2 * halo)],
        in_specs=[HBM],
        out_specs=[VMEM] * 2,
        scratch_shapes=[pltpu.SemaphoreType.DMA((3,))],
        compiler_params=params(44),
    )(panel)


def load_kernel(*refs):
    count = len(refs) // 2
    sources, targets, sems = refs[:count], refs[count:2 * count], refs[-1]
    copies = []
    for which, (source, target) in enumerate(zip(sources, targets)):
        size = source.shape[0] // 4
        for part in range(4):
            span = pl.ds(part * size, size if part < 3 else source.shape[0] - 3 * size)
            copies.append(pltpu.make_async_copy(source.at[span], target.at[span], sems.at[which, part]))
    for copy in copies:
        copy.start()
    for copy in copies:
        copy.wait()


def load(*arrays):
    size = sum(array.size * array.dtype.itemsize for array in arrays)
    return pl.pallas_call(
        load_kernel,
        out_shape=[shape(array.shape, array.dtype) for array in arrays],
        in_specs=[HBM] * len(arrays),
        out_specs=[VMEM] * len(arrays),
        scratch_shapes=[pltpu.SemaphoreType.DMA((len(arrays), 4))],
        compiler_params=params(45),
        cost_estimate=pl.CostEstimate(flops=0, bytes_accessed=size * 1, transcendentals=0),
    )(*arrays)


def project_kernel(spans, places, groups, more, *refs):
    ids_ref, g_ref, c_ref, basis_ref = refs[:4]
    pieces = refs[4:4 + 2 * len(places)]
    rest = list(refs[4 + 2 * len(places):])
    before = rest.pop(0) if more else None
    *outs, ext, prods = rest
    slots = g_ref.shape[1]
    width = ROWS_OF_CORE
    core = lax.axis_index("col") % 2
    odd = lax.axis_index("node") % 2

    for which, (bases, parts) in enumerate(places):
        for owner, base, ref in zip((core, 1 - core), bases, pieces[2 * which:2 * which + 2]):
            at = pl.ds(pl.multiple_of(owner * width, width), width)
            for source, even_target, odd_target, count in parts:
                target = even_target
                if odd_target != even_target:
                    target = pl.multiple_of(even_target + odd * (odd_target - even_target), BS)
                ext[at, pl.ds(target, count)] = ref[base:base + width, source:source + count]

    at = 0
    total = None
    for lo, hi in spans:
        begin = at
        for row in range(lo, hi):
            near = jnp.concatenate(
                [ext[:, pl.ds(pl.multiple_of(ids_ref[slot, row] * BS, BS), BS)] for slot in range(slots)], axis=1
            )
            both = jnp.concatenate(
                [jnp.concatenate([ref[row, slot] for slot in range(slots)], axis=1) for ref in (g_ref, c_ref)], axis=0
            )
            prod = lax.dot_general(both, near, (((1,), (1,)), ((), ())), preferred_element_type=F32).astype(BF16)
            prods[at:at + BS, 0:2 * width] = prod[0:BS]
            prods[at:at + BS, 2 * width:4 * width] = prod[BS:2 * BS]
            at += BS
        part = lax.dot_general(
            basis_ref[lo * BS:hi * BS, :], prods[begin:at, :], (((0,), (0,)), ((), ())), preferred_element_type=F32
        )
        total = part if total is None else total + part
    if before is not None:
        total = total + before[...]
    if len(outs) == 1:
        outs[0][...] = total
        return
    send_ref, keep_ref = outs
    states, columns = total.shape
    total = total.reshape(groups, 2, states // (2 * groups), columns)
    keep_ref[...] = jnp.where(odd == 1, total[:, 1], total[:, 0])
    send_ref[...] = jnp.where(odd == 1, total[:, 0], total[:, 1]).astype(BF16)


def project(fixed, pieces, spans, groups, before=None, last=True):
    ids, g_blocks, c_blocks, basis = fixed
    rows, slots = g_blocks.shape[0], g_blocks.shape[1]
    width = ROWS_OF_CORE
    states = basis.shape[1]
    piece = (groups, states // (2 * groups), 4 * width)
    arrays = [array for mine, other, _, _ in pieces for array in (mine, other)]
    more = [] if before is None else [before]
    count = sum(hi - lo for lo, hi in spans)
    outs = [shape(piece, BF16), shape(piece, F32)] if last else [shape((states, 4 * width), F32)]
    places = [(base, parts) for _, _, base, parts in pieces]
    return pl.pallas_call(
        functools.partial(project_kernel, spans, places, groups, before is not None),
        out_shape=outs,
        in_specs=[SMEM] + [VMEM] * (3 + len(arrays) + len(more)),
        out_specs=[VMEM] * len(outs),
        scratch_shapes=[
            pltpu.VMEM((2 * width, (rows + 2 * HB) * BS), BF16),
            pltpu.VMEM((count * BS, 4 * width), BF16),
        ],
        compiler_params=params(14),
        cost_estimate=pl.CostEstimate(flops=int(3.45e+09) if more else (count if last else int(1)), bytes_accessed=count, transcendentals=0),
    )(ids, g_blocks, c_blocks, basis, *arrays, *more)


def spread_kernel(groups, keep, got, keep_ref, *send_refs):
    here = lax.axis_index("node") // 2
    for step in range(groups):
        value = keep[here ^ step] + got[here ^ step].astype(F32)
        if step == 0:
            keep_ref[...] = value
        else:
            send_refs[step - 1][...] = value.astype(BF16)


def spread(groups, keep, got):
    piece = keep.shape[1:]
    return pl.pallas_call(
        functools.partial(spread_kernel, groups),
        out_shape=[shape(piece, F32)] + [shape(piece, BF16)] * (groups - 1),
        in_specs=[VMEM] * 2,
        out_specs=[VMEM] * groups,
        compiler_params=params(4),
    )(keep, got)


def finish_kernel(count, *refs):
    out_g, out_c = refs[-2:]
    quarter = out_g.shape[1] // 2
    first = lax.axis_index("col") // 2
    for place, half in ((first, refs[:count]), (1 - first, refs[count:2 * count])):
        total = half[0][...]
        for ref in half[1:]:
            total = total + ref[...].astype(F32)
        at = pl.ds(pl.multiple_of(place * quarter, quarter), quarter)
        out_g[:, at] = total[:, 0:quarter]
        out_c[:, at] = total[:, quarter:2 * quarter]


def finish(own, far):
    piece = shape(own[0].shape, F32)
    return pl.pallas_call(
        functools.partial(finish_kernel, len(own)),
        out_shape=(piece, piece),
        in_specs=[VMEM] * (len(own) + len(far)),
        out_specs=(VMEM, VMEM),
        compiler_params=params(4),
    )(*own, *far)


def body(panel, basis, g_blocks, c_blocks, block_cols):
    nodes, cols = lax.axis_size("node"), lax.axis_size("col")
    rows = g_blocks.shape[0]
    groups = nodes // 2
    halo = HB * BS
    inner = rows * BS

    def across(array):
        return lax.ppermute(array, "col", [(i, i ^ 2) for i in range(cols)])

    def cores(array):
        return lax.ppermute(array, "col", [(i, i ^ 1) for i in range(cols)])

    def swap(array, step):
        return lax.ppermute(array, "node", [(i, i ^ step) for i in range(nodes)])

    def swap_next(array):
        pairs = [(i, i + 1) for i in range(1, nodes - 1, 2)]
        return lax.ppermute(array, "node", pairs + [(j, i) for i, j in pairs])

    ends, middle = cut(panel.T)
    far_ends, far_middle = across(ends), across(middle)
    ends_other = cores(ends)
    own = [
        (ends, ends_other, (0, 0), [(0, inner, halo, halo), (halo, halo, inner, halo)]),
        (middle, cores(middle), (0, 0), [(0, 2 * halo, 2 * halo, inner - 2 * halo)]),
    ]
    (basis,) = load(basis)
    ids = jnp.clip(block_cols.T - (lax.axis_index("node") * rows - HB), 0, rows + 2 * HB - 1)
    far_ends, basis, ids = lax.optimization_barrier((far_ends, basis, ids))
    all_ends = jnp.concatenate([ends, ends_other, far_ends], axis=0)
    rim = jnp.concatenate([swap(all_ends[:, :halo], 1), swap_next(all_ends[:, halo:])], axis=1)
    fixed = (ids, g_blocks, c_blocks, basis)
    (part,) = project(fixed, own, [(HB, rows - HB)], groups, last=False)
    part, far_middle = lax.optimization_barrier((part, far_middle))
    far_rim = 2 * ROWS_OF_CORE
    near_parts = [(0, 2 * halo, 2 * halo, halo), (inner - 3 * halo, inner - halo, inner - halo, halo)]
    near_rim = [own[0], own[1][:3] + (near_parts,)]
    rim_parts = [(0, halo + inner, 0, halo), (halo, 0, halo + inner, halo)]
    send_a, keep_a = project(
        fixed, near_rim + [(rim, rim, (0, ROWS_OF_CORE), rim_parts)], [(0, HB), (rows - HB, rows)], groups, before=part
    )
    got_a = swap(send_a, 1)
    far = [
        (rim, cores(rim[far_rim:]), (far_rim, 0), rim_parts),
        (far_ends, cores(far_ends), (0, 0), [(0, inner, halo, halo), (halo, halo, inner, halo)]),
        (far_middle, cores(far_middle), (0, 0), [(0, 2 * halo, 2 * halo, inner - 2 * halo)]),
    ]
    send_b, keep_b = project(fixed, far, [(0, rows)], groups)
    got_b = swap(send_b, 1)
    halves = []
    for keep, got in ((keep_a, got_a), (keep_b, got_b)):
        keep, *sends = spread(groups, keep, got)
        steps = sorted(range(1, groups), key=lambda step: -step)
        halves.append([keep] + [swap(sends[step - 1], 2 * step) for step in steps])
    return finish(*halves)


def solution(mesh):
    in_specs = (
        P("node", "col"),
        P("node", "col"),
        P("node", None, None, None),
        P("node", None, None, None),
        P("node", None),
    )
    out_specs = (P(("col", "node"), None), P(("col", "node"), None))
    return jax.shard_map(body, mesh=mesh, in_specs=in_specs, out_specs=out_specs, check_vma=False)
```
